32 devices in a mesh: pipe: 4 (over y, x), tensor: 8 (over z, core).
Axes of the slice: x: 2, y: 2, z: 4, core: 2. Of those that a mesh axis runs over, the one named last changes fastest.
Arguments:
- layer_input: bfloat16 [768, 8192], P('tensor', 'pipe'), may hold values from -6 to 6
- out_grad: bfloat16 [768, 8192], P('tensor', 'pipe'), may hold values from -2 to 2
- gate_pre: bfloat16 [768, 28672], P(None, 'tensor'), may hold values from -8 to 8
- up_pre: bfloat16 [768, 28672], P(None, 'tensor'), may hold values from -6 to 6
- gate_weight: bfloat16 [8192, 28672], P('pipe', 'tensor'), may hold values from -0.0625 to 0.0625
- up_weight: bfloat16 [8192, 28672], P('pipe', 'tensor'), may hold values from -0.0625 to 0.0625
- down_weight: bfloat16 [28672, 8192], P('tensor', 'pipe'), may hold values from -0.03125 to 0.03125
- gate_mask: int32 [64, 224], P('pipe', 'tensor'), may hold values from 0 to 1, as said below
- up_mask: int32 [64, 224], P('pipe', 'tensor'), may hold values from 0 to 1, as said below
- down_mask: int32 [224, 64], P('tensor', 'pipe'), may hold values from 0 to 1, as said below
Outputs:
- grad_input: bfloat16 [768, 8192], P('tensor', 'pipe')
- grad_gate: bfloat16 [8192, 28672], P('pipe', 'tensor')
- grad_up: bfloat16 [8192, 28672], P('pipe', 'tensor')
- grad_down: bfloat16 [28672, 8192], P('tensor', 'pipe')
The draws below stay inside these ranges and needn't reach their ends.
Inputs may be any that keep to these rules, and one draw needn't show every extreme that they name: `gate_mask`: each entry is 1 for a kept block and 0 for a pruned one; the share of kept blocks differs from block column to block column. `up_mask`: each entry is 1 for a kept block and 0 for a pruned one; the share of kept blocks differs from block column to block column. `down_mask`: each entry is 1 for a kept block and 0 for a pruned one; the share of kept blocks differs from block row to block row.
All inputs are finite; a program needn't handle non-finite values.
Results may differ from the reference program's by a relative error of at most 0.005.
Values may be sent and summed in bfloat16 or wider, within the bound.
No kernel may reach another device: no remote copies, remote signals or barrier semaphores. Data moves between devices by JAX's collectives and lax.ppermute only.
A program may use at most 256 MiB of HBM per device.

```python
import jax
import jax.numpy as jnp
from jax import lax

D = 8192
FF = 28672
BLOCK = 128
TOKENS = 768


def block_mask(key, rows, cols, by_rows):
    level_key, value_key = jax.random.split(key)
    if by_rows:
        level = jax.random.randint(level_key, (rows, 1), 1, 8)
    else:
        level = jax.random.randint(level_key, (1, cols), 1, 8)
    values = jax.random.randint(value_key, (rows, cols), 0, 8)
    return (values < level).astype(jnp.int32)


def draw_gate_mask(key, part):
    return block_mask(jax.random.fold_in(key, 11), D // BLOCK, FF // BLOCK, False)


def draw_up_mask(key, part):
    return block_mask(jax.random.fold_in(key, 23), D // BLOCK, FF // BLOCK, False)


def draw_down_mask(key, part):
    return block_mask(jax.random.fold_in(key, 37), FF // BLOCK, D // BLOCK, True)


def steps_of(stream_key, shape, cuts, low, largest):
    def one(position, shards_of):
        steps = jax.random.uniform(jax.random.fold_in(jax.random.fold_in(stream_key, 6), position), (shards_of,), jnp.float32, low / len(cuts), largest / len(cuts))
        return jnp.repeat(jnp.exp(steps), shape[position] // shards_of).reshape((-1,) + (1,) * (len(shape) - position - 1))

    factor_of = one(*cuts[0])
    for cut in cuts[1:]:
        factor_of = factor_of * one(*cut)
    return factor_of


def normal_values(rng, extent, scale, bound, cuts=(), kind=jnp.bfloat16):
    values = scale * jax.random.normal(rng, extent, jnp.float32)
    if cuts:
        values = values * steps_of(rng, extent, cuts, -0.22, 0.18)
    return jnp.clip(values, -bound, bound).astype(kind)


def setup_inputs(seed: int = 0) -> dict:
    keys = jax.random.split(jax.random.key(seed), 11)
    return {
        "layer_input": normal_values(keys[0], (TOKENS, D), 1.0, 6.0, ((0, 8), (1, 4))),
        "out_grad": normal_values(keys[1], (TOKENS, D), 0.25, 2.0, ((0, 8), (1, 4))),
        "gate_pre": normal_values(keys[2], (TOKENS, FF), 1.5, 8.0, ((1, 8),)),
        "up_pre": normal_values(keys[3], (TOKENS, FF), 1.0, 6.0, ((1, 8),)),
        "gate_weight": normal_values(keys[4], (D, FF), D ** -0.5, 0.0625, ((0, 4), (1, 8))),
        "up_weight": normal_values(keys[5], (D, FF), D ** -0.5, 0.0625, ((0, 4), (1, 8))),
        "down_weight": normal_values(keys[6], (FF, D), FF ** -0.5, 0.03125, ((0, 8), (1, 4))),
        "gate_mask": draw_gate_mask(jax.random.fold_in(keys[10], 71), 0),
        "up_mask": draw_up_mask(jax.random.fold_in(keys[10], 71), 0),
        "down_mask": draw_down_mask(jax.random.fold_in(keys[10], 71), 0),
    }


def expand(mask):
    return jnp.repeat(jnp.repeat(mask, BLOCK, axis=0), BLOCK, axis=1)


def reference(layer_input, out_grad, gate_pre, up_pre, gate_weight, up_weight, down_weight, gate_mask, up_mask, down_mask):
    slab_count = 16
    width = FF // slab_count
    nblocks = width // BLOCK

    def split_cols(array, per):
        return array.reshape(array.shape[0], slab_count, per).transpose(1, 0, 2)

    items = (split_cols(gate_weight, width), split_cols(up_weight, width), down_weight.reshape(slab_count, width, D),
             split_cols(gate_mask, nblocks), split_cols(up_mask, nblocks), down_mask.reshape(slab_count, nblocks, D // BLOCK),
             split_cols(gate_pre, width), split_cols(up_pre, width))

    def one_slab(carry, slab):
        wg_s, wu_s, wd_s, mg_s, mu_s, md_s, gp_s, up_s = slab
        mask_gate = expand(mg_s)
        mask_up = expand(mu_s)
        mask_down = expand(md_s)
        gate_masked = wg_s * mask_gate.astype(jnp.bfloat16)
        up_masked = wu_s * mask_up.astype(jnp.bfloat16)
        down_masked = wd_s * mask_down.astype(jnp.bfloat16)
        hidden_grad = jnp.dot(out_grad, down_masked.T, preferred_element_type=jnp.float32)
        gate_val = gp_s.astype(jnp.float32)
        up_val = up_s.astype(jnp.float32)
        sigma_val = jax.nn.sigmoid(gate_val)
        hidden = (gate_val * sigma_val * up_val).astype(jnp.bfloat16)
        grad_down = (jnp.dot(hidden.T, out_grad, preferred_element_type=jnp.float32) * mask_down.astype(jnp.float32)).astype(jnp.bfloat16)
        gate_grad = (hidden_grad * up_val * sigma_val * (1.0 + gate_val * (1.0 - sigma_val))).astype(jnp.bfloat16)
        up_grad = (hidden_grad * gate_val * sigma_val).astype(jnp.bfloat16)
        grad_gate = (jnp.dot(layer_input.T, gate_grad, preferred_element_type=jnp.float32) * mask_gate.astype(jnp.float32)).astype(jnp.bfloat16)
        grad_up = (jnp.dot(layer_input.T, up_grad, preferred_element_type=jnp.float32) * mask_up.astype(jnp.float32)).astype(jnp.bfloat16)
        carry = carry + jnp.dot(gate_grad, gate_masked.T, preferred_element_type=jnp.float32)
        carry = carry + jnp.dot(up_grad, up_masked.T, preferred_element_type=jnp.float32)
        return carry, (grad_gate, grad_up, grad_down)

    total, (grad_gate, grad_up, grad_down) = lax.scan(one_slab, jnp.zeros((TOKENS, D), jnp.float32), items)
    grad_gate = grad_gate.transpose(1, 0, 2).reshape(D, FF)
    grad_up = grad_up.transpose(1, 0, 2).reshape(D, FF)
    grad_down = grad_down.reshape(FF, D)
    return (total.astype(jnp.bfloat16), grad_gate, grad_up, grad_down)
```

```python
import functools

import jax
import jax.numpy as jnp
from jax import lax
from jax.experimental import pallas as pl
from jax.experimental.pallas import tpu as pltpu
from jax.sharding import PartitionSpec as P

BLOCK = 128
COLS = 256
BF16 = jnp.bfloat16
F32 = jnp.float32
VMEM_BYTES = 60 * 1024 * 1024
NT = (((1,), (1,)), ((), ()))
NN = (((1,), (0,)), ((), ()))


def params():
    return pltpu.CompilerParams(vmem_limit_bytes=VMEM_BYTES)


def ring_of(chips):
    return [0] + list(range(1, chips, 2)) + [c for c in range(chips - 1, 0, -1) if c % 2 == 0]


class Axes:
    def __init__(self, mesh):
        self.pipe = mesh.shape["pipe"]
        self.tensor = mesh.shape["tensor"]
        self.chips = self.tensor // 2
        ring = ring_of(self.chips)
        table = [[ring[(ring.index(c) - s) % self.chips] for s in range(self.chips)] for c in range(self.chips)]
        self.ring = ring
        self.table = table

    def scalars(self):
        me = lax.axis_index("tensor")
        slots = lax.dynamic_slice(jnp.array(self.table, jnp.int32), (me // 2, 0), (1, self.chips))[0]
        head = jnp.stack([lax.axis_index("pipe"), me % 2]).astype(jnp.int32)
        return jnp.concatenate([head, slots])

    def to_core(self, x):
        return lax.ppermute(x, "tensor", [(t, t ^ 1) for t in range(self.tensor)])

    def to_next(self, x):
        pairs = [(self.ring[i], self.ring[(i + 1) % self.chips]) for i in range(self.chips)]
        return lax.ppermute(x, "tensor", [(2 * a + k, 2 * b + k) for a, b in pairs for k in range(2)])

    def to_pipe(self, x, bit):
        return lax.ppermute(x, "pipe", [(i, i ^ bit) for i in range(self.pipe)])


def place_in(index, order):
    out = 0
    for bit in order:
        out = out * 2 + (1 if index & bit else 0)
    return out


def partial_kernel(cfg, scal, *refs):
    own, sib = refs[: cfg["slots"]], refs[cfg["slots"] : 2 * cfg["slots"]]
    down, mask = refs[2 * cfg["slots"] : 2 * cfg["slots"] + 2]
    outs = refs[2 * cfg["slots"] + 2 : -1]
    rows = refs[-1]
    step = pl.program_id(0)
    pipe, part, tok, unit = cfg["pipe"], cfg["part"], cfg["tok"], cfg["unit"]

    @pl.when(step == 0)
    def _():
        place, core = scal[0], scal[1]
        for s in range(cfg["slots"]):
            for ref, which in ((own[s], core), (sib[s], 1 - core)):
                for h in range(tok // unit):
                    at = (2 * s + which) * tok + h * unit
                    quarter = lax.div(at, part)
                    to = (quarter ^ place) * part + (at - quarter * part)
                    rows[pl.ds(pl.multiple_of(to, 16), unit), :] = ref[h * unit : (h + 1) * unit, :]

    kept = [down[i * BLOCK : (i + 1) * BLOCK, :] * mask[i].astype(BF16) for i in range(COLS // BLOCK)]
    acc = lax.dot_general(rows[...], jnp.concatenate(kept, axis=0), NT, preferred_element_type=F32)
    half = pipe // 2
    first = 0
    for i, (order, steps) in enumerate(cfg["subs"]):
        send, keep = outs[2 * i], outs[2 * i + 1]

        def store(send=send, keep=keep, order=order):
            for r in range(pipe):
                to = place_in(r, order)
                block = acc[r * part : (r + 1) * part, :]
                if to >= half:
                    send[to - half] = block.astype(BF16)
                else:
                    keep[to] = block

        if len(cfg["subs"]) == 1:
            store()
        else:
            pl.when((step >= first) & (step < first + steps))(store)
        first += steps


def partial_sums(axes, scal, own, sib, down, mask, subs):
    tok, width = own[0].shape
    slots = len(own)
    rows = 2 * slots * tok
    part = rows // axes.pipe
    unit = max(u for u in (16, 32, 48, 96, 144) if tok % u == 0 and part % u == 0)
    start = subs[0][0] // COLS
    steps = sum(w for _, w, _ in subs) // COLS
    half = axes.pipe // 2
    cfg = dict(slots=slots, pipe=axes.pipe, part=part, tok=tok, unit=unit, subs=[(o, w // COLS) for _, w, o in subs])
    shapes, specs = [], []
    first = 0
    for _, w, _ in subs:
        n = w // COLS

        def where(k, _, first=first, n=n):
            return (0, 0, jnp.clip(k - first, 0, n - 1))

        for kind in (BF16, F32):
            shapes.append(jax.ShapeDtypeStruct((half, part, w), kind))
            specs.append(pl.BlockSpec((half, part, COLS), where))
        first += n
    whole = pl.BlockSpec((tok, width), lambda k, _: (0, 0))
    blocks = COLS // BLOCK
    out = pl.pallas_call(
        functools.partial(partial_kernel, cfg),
        out_shape=shapes,
        grid_spec=pltpu.PrefetchScalarGridSpec(
            num_scalar_prefetch=1,
            grid=(steps,),
            in_specs=[whole] * (2 * slots)
            + [
                pl.BlockSpec((COLS, width), lambda k, _: (start + k, 0)),
                pl.BlockSpec((blocks, 1, width), lambda k, _: (start + k, 0, 0)),
            ],
            out_specs=specs,
            scratch_shapes=[pltpu.VMEM((rows, width), BF16)],
        ),
        compiler_params=params(),
        cost_estimate=pl.CostEstimate(
            flops=2 * rows * width * steps * COLS,
            bytes_accessed=2 * (rows * width + width * steps * COLS) + 3 * rows * steps * COLS,
            transcendentals=0,
        ),
        name="partial_sums",
    )(scal, *own, *sib, down, mask)
    return [(out[2 * i], out[2 * i + 1]) for i in range(len(subs))]


def reduce_over_pipe(axes, send, keep, order):
    count = axes.pipe // 2
    for bit in order:
        total = keep + axes.to_pipe(send, bit).astype(F32)
        count //= 2
        if count:
            send, keep = total[count:].astype(BF16), total[:count]
    held = {0: total[0].astype(BF16)}
    for bit in reversed(order):
        for r in list(held):
            held[r ^ bit] = axes.to_pipe(held[r], bit)
    return [held[r] for r in range(axes.pipe)]


def grads_kernel(cfg, scal, *refs):
    refs = list(refs)
    sources = []
    for src in cfg["sources"]:
        sources.append([refs.pop(0) for _ in range(cfg["pipe"])])
    gate_pre, up_pre, gate_w, up_w, gate_m, up_m = [refs.pop(0) for _ in range(6)]
    acc_in = refs.pop(0) if cfg["acc_in"] else None
    gate_out, up_out = refs.pop(0), refs.pop(0)
    if cfg["last"]:
        mine = [refs.pop(0) for _ in range(cfg["chips"])]
        theirs = refs.pop(0)
    else:
        acc_out = refs.pop(0)
    hidden, both, acc = refs
    step = pl.program_id(0)
    place, core = scal[0], scal[1]
    per = 2 * cfg["tok"]

    for src, arrays in zip(cfg["sources"], sources):

        def copy(src=src, arrays=arrays):
            for r in range(cfg["pipe"]):
                to = src["base"] + (place ^ r) * src["part"]
                hidden[pl.ds(pl.multiple_of(to, 16), src["part"]), :] = arrays[r][...]

        if src["lo"] <= 0 and src["hi"] >= cfg["steps"]:
            copy()
        else:
            pl.when((step >= src["lo"]) & (step < src["hi"]))(copy)

    for s in range(cfg["chips"]):
        at = pl.ds(pl.multiple_of(scal[2 + s] * per, 16), per)
        rows = slice(s * per, (s + 1) * per)
        g = gate_pre[at, :].astype(F32)
        u = up_pre[at, :].astype(F32)
        h = hidden[rows, :].astype(F32)
        sig = 1.0 / (1.0 + jnp.exp(-g))
        gg = (h * u * sig * (1.0 + g * (1.0 - sig))).astype(BF16)
        ug = (h * g * sig).astype(BF16)
        gate_out[rows, :] = gg
        up_out[rows, :] = ug
        both[rows, :COLS] = gg
        both[rows, COLS:] = ug

    def tile(n, first):
        def masked(w, m):
            two = []
            for i in range(COLS // BLOCK):
                at = pl.ds(pl.multiple_of(n * COLS + i * BLOCK, BLOCK), BLOCK)
                two.append(w[at, :] * m[pl.ds(n * (COLS // BLOCK) + i, 1), :].astype(BF16))
            return jnp.concatenate(two, axis=0)

        w = jnp.concatenate([masked(gate_w, gate_m), masked(up_w, up_m)], axis=1)
        to = pl.ds(pl.multiple_of(n * COLS, COLS), COLS)
        term = lax.dot_general(both[...], w, NT, preferred_element_type=F32)
        if first:
            acc[:, to] = term
        else:
            acc[:, to] += term

    tiles = cfg["width"] // COLS

    @pl.when(step == 0)
    def _():
        pl.loop(0, tiles)(lambda n: tile(n, True))

    @pl.when(step > 0)
    def _():
        pl.loop(0, tiles)(lambda n: tile(n, False))

    @pl.when(step == cfg["steps"] - 1)
    def _():
        tok = cfg["tok"]
        if not cfg["last"]:
            acc_out[...] = acc[...] + acc_in[...] if cfg["acc_in"] else acc[...]
            return

        def take(s, which):
            at = pl.ds(pl.multiple_of(s * per + which * tok, 16), tok)
            return acc[at, :] + acc_in[at, :] if cfg["acc_in"] else acc[at, :]

        for s in range(cfg["chips"]):
            mine[s][...] = take(s, core)
            theirs[s] = take(s, 1 - core).astype(BF16)


def grads(axes, scal, sources, gate_pre, up_pre, gate_w, up_w, gate_m, up_m, acc, start, cols, last):
    tokens = gate_pre.shape[0]
    width = gate_w.shape[0]
    tok = tokens // axes.tensor
    steps = cols // COLS
    first = start // COLS
    infos, specs, arrays = [], [], []
    for parts, base, part, c0, w in sources:
        lo, n = (c0 - start) // COLS, w // COLS
        infos.append(dict(base=base, part=part, lo=lo, hi=lo + n))
        for a in parts:
            arrays.append(a)
            specs.append(pl.BlockSpec((part, COLS), lambda k, _, lo=lo, n=n: (0, jnp.clip(k - lo, 0, n - 1))))
    col = lambda k, _: (0, first + k)
    one = lambda k, _: (0, 0)
    specs += [pl.BlockSpec((tokens, COLS), col)] * 2
    specs += [pl.BlockSpec((width, COLS), col)] * 2
    specs += [pl.BlockSpec((gate_m.shape[0], COLS), col)] * 2
    arrays += [gate_pre, up_pre, gate_w, up_w, gate_m, up_m]
    if acc is not None:
        specs.append(pl.BlockSpec((tokens, width), one, pipeline_mode=pl.Buffered(1)))
        arrays.append(acc)
    shapes = [jax.ShapeDtypeStruct((tokens, cols), BF16)] * 2
    out_specs = [pl.BlockSpec((tokens, COLS), lambda k, _: (0, k))] * 2
    if last:
        shapes += [jax.ShapeDtypeStruct((tok, width), F32)] * axes.chips
        out_specs += [pl.BlockSpec((tok, width), one)] * axes.chips
        shapes.append(jax.ShapeDtypeStruct((axes.chips, tok, width), BF16))
        out_specs.append(pl.BlockSpec((axes.chips, tok, width), lambda k, _: (0, 0, 0)))
    else:
        shapes.append(jax.ShapeDtypeStruct((tokens, width), F32))
        out_specs.append(pl.BlockSpec((tokens, width), one))
    cfg = dict(
        sources=infos, pipe=axes.pipe, chips=axes.chips, tok=tok, steps=steps, width=width, last=last,
        acc_in=acc is not None,
    )
    return pl.pallas_call(
        functools.partial(grads_kernel, cfg),
        out_shape=shapes,
        grid_spec=pltpu.PrefetchScalarGridSpec(
            num_scalar_prefetch=1,
            grid=(steps,),
            in_specs=specs,
            out_specs=out_specs,
            scratch_shapes=[
                pltpu.VMEM((tokens, COLS), BF16),
                pltpu.VMEM((tokens, 2 * COLS), BF16),
                pltpu.VMEM((tokens, width), F32),
            ],
        ),
        compiler_params=params(),
        cost_estimate=pl.CostEstimate(
            flops=4 * tokens * width * cols,
            bytes_accessed=4 * width * cols + 10 * tokens * cols + 8 * tokens * width,
            transcendentals=tokens * cols,
        ),
        name="hidden_grads",
    )(scal, *arrays)


def weights_kernel(cfg, x, gate, up, gate_m, up_m, *refs):
    outs = refs[-2:]
    chunk = cfg["chunk"]
    for g, m, out in ((gate, gate_m, outs[0]), (up, up_m, outs[1])):

        def tile(n, g=g, m=m, out=out):
            at = pl.ds(pl.multiple_of(n * chunk, chunk), chunk)
            term = lax.dot_general(x[at, :], g[...], NN, preferred_element_type=F32)
            for i in range(chunk // BLOCK):
                to = pl.ds(pl.multiple_of(n * chunk + i * BLOCK, BLOCK), BLOCK)
                row = m[pl.ds(n * (chunk // BLOCK) + i, 1), :]
                out[to, :] = (term[i * BLOCK : (i + 1) * BLOCK, :] * row).astype(BF16)

        pl.loop(0, cfg["width"] // chunk)(tile)


def weight_grads(x_t, gate, up, gate_m, up_m, before, shape, start):
    width, tokens = x_t.shape
    steps = gate.shape[1] // COLS
    first = start // COLS
    chunk = 512 if width % 512 == 0 else BLOCK
    col = lambda k: (0, first + k)
    specs = [
        pl.BlockSpec((width, tokens), lambda k: (0, 0), pipeline_mode=pl.Buffered(1)),
        pl.BlockSpec((tokens, COLS), lambda k: (0, k)),
        pl.BlockSpec((tokens, COLS), lambda k: (0, k)),
        pl.BlockSpec((gate_m.shape[0], COLS), col),
        pl.BlockSpec((gate_m.shape[0], COLS), col),
    ]
    arrays = [x_t, gate, up, gate_m, up_m]
    alias = {}
    if before is not None:
        specs += [pl.BlockSpec(memory_space=pl.ANY)] * 2
        arrays += list(before)
        alias = {5: 0, 6: 1}
    return pl.pallas_call(
        functools.partial(weights_kernel, dict(width=width, chunk=chunk)),
        out_shape=[jax.ShapeDtypeStruct(shape, BF16)] * 2,
        grid=(steps,),
        in_specs=specs,
        out_specs=[pl.BlockSpec((width, COLS), col)] * 2,
        input_output_aliases=alias,
        compiler_params=params(),
        cost_estimate=pl.CostEstimate(
            flops=4 * tokens * width * steps * COLS,
            bytes_accessed=4 * (width + tokens) * steps * COLS + 2 * tokens * width,
            transcendentals=0,
        ),
        name="weight_grads",
    )(*arrays)


def down_kernel(cfg, scal, *refs):
    chips, tok = cfg["chips"], cfg["tok"]
    own, sib = refs[:chips], refs[chips : 2 * chips]
    gate_pre, up_pre, mask, out, rows = refs[2 * chips :]
    core = scal[1]
    per = 2 * tok

    @pl.when(pl.program_id(0) == 0)
    def _():
        for s in range(chips):
            base = scal[2 + s] * per
            for ref, which in ((own[s], core), (sib[s], 1 - core)):
                rows[pl.ds(pl.multiple_of(base + which * tok, 16), tok), :] = ref[...]

    g = gate_pre[...].astype(F32)
    u = up_pre[...].astype(F32)
    hidden = (g * (1.0 / (1.0 + jnp.exp(-g))) * u).astype(BF16).T
    chunk = cfg["chunk"]

    def tile(n):
        at = pl.ds(pl.multiple_of(n * chunk, chunk), chunk)
        term = lax.dot_general(hidden, rows[:, at], NN, preferred_element_type=F32)
        for i in range(COLS // BLOCK):
            part = slice(i * BLOCK, (i + 1) * BLOCK)
            out[part, at] = (term[part, :] * mask[i, :, at]).astype(BF16)

    pl.loop(0, cfg["width"] // chunk)(tile)


def down_grad(axes, scal, own, sib, gate_pre, up_pre, mask):
    tokens, hid = gate_pre.shape
    tok, width = own[0].shape
    whole = pl.BlockSpec((tok, width), lambda k, _: (0, 0), pipeline_mode=pl.Buffered(1))
    blocks = COLS // BLOCK
    cfg = dict(chips=axes.chips, tok=tok, width=width, chunk=512 if width % 512 == 0 else BLOCK)
    return pl.pallas_call(
        functools.partial(down_kernel, cfg),
        out_shape=jax.ShapeDtypeStruct((hid, width), BF16),
        grid_spec=pltpu.PrefetchScalarGridSpec(
            num_scalar_prefetch=1,
            grid=(hid // COLS,),
            in_specs=[whole] * (2 * axes.chips)
            + [pl.BlockSpec((tokens, COLS), lambda k, _: (0, k))] * 2
            + [pl.BlockSpec((blocks, 1, width), lambda k, _: (k, 0, 0))],
            out_specs=pl.BlockSpec((COLS, width), lambda k, _: (k, 0)),
            scratch_shapes=[pltpu.VMEM((tokens, width), BF16)],
        ),
        compiler_params=params(),
        cost_estimate=pl.CostEstimate(
            flops=2 * tokens * width * hid,
            bytes_accessed=2 * (tokens * width + 2 * tokens * hid + width * hid),
            transcendentals=tokens * hid,
        ),
        name="down_grad",
    )(scal, *own, *sib, gate_pre, up_pre, mask)


def gather(axes, x):
    own = [x]
    for _ in range(axes.chips - 1):
        own.append(axes.to_next(own[-1]))
    return own, [axes.to_core(a) for a in own]


def pieces_of(hid, orders):
    pieces, at = [], 0
    while at < hid:
        width = min(1024, hid - at)
        half = width // 2 // COLS * COLS
        if half:
            pieces.append([(at, half, orders[0]), (at + half, width - half, orders[1])])
        else:
            pieces.append([(at, width, orders[0])])
        at += width
    return pieces


def shards(axes, layer_input, out_grad, gate_pre, up_pre, gate_weight, up_weight, down_weight, gate_mask, up_mask, down_mask):
    tokens, hid = gate_pre.shape
    tok = out_grad.shape[0]
    scal = axes.scalars()
    gate_m = jnp.repeat(gate_mask, BLOCK, axis=1).astype(F32)
    up_m = jnp.repeat(up_mask, BLOCK, axis=1).astype(F32)
    down_m = jnp.repeat(down_mask, BLOCK, axis=1).astype(F32)[:, None, :]

    bits = [1 << i for i in range(axes.pipe.bit_length() - 1)]
    orders = [bits, bits[::-1]]
    own, sib = gather(axes, out_grad)
    x_own, x_sib = gather(axes, lax.optimization_barrier((layer_input, own[-1]))[0])

    early = 1 if (2 * tok) % (16 * axes.pipe) == 0 and axes.chips > 1 else 0
    pieces = pieces_of(hid, orders)
    sources = []
    if early:
        part = 2 * tok // axes.pipe
        split = sum(w for _, w, _ in pieces[0] + (pieces[1] if len(pieces) > 1 else []))
        subs = [(0, split, orders[0])] + ([(split, hid - split, orders[1])] if split < hid else [])
        for sub in subs:
            send, keep = partial_sums(axes, scal, own[:1], sib[:1], down_weight, down_m, [sub])[0]
            sources.append((reduce_over_pipe(axes, send, keep, sub[2]), 0, part, sub[0], sub[1]))
    part = (tokens - early * 2 * tok) // axes.pipe
    late = []
    for subs in pieces:
        sums = partial_sums(axes, scal, own[early:], sib[early:], down_weight, down_m, subs)
        late.append(
            [
                (reduce_over_pipe(axes, send, keep, sub[2]), early * 2 * tok, part, sub[0], sub[1])
                for (send, keep), sub in zip(sums, subs)
            ]
        )

    grad_down = down_grad(axes, scal, own, sib, gate_pre, up_pre, down_m)
    core = lax.axis_index("tensor") % 2
    ordered = []
    for a, b in zip(x_own, x_sib):
        ordered += [jnp.where(core == 0, a, b), jnp.where(core == 0, b, a)]
    x_t = jnp.concatenate(ordered, axis=0).T

    acc, weights = None, None
    for i, subs in enumerate(pieces):
        start, cols = subs[0][0], sum(w for _, w, _ in subs)
        using = [s for s in sources if s[3] < start + cols and s[3] + s[4] > start] + late[i]
        last = i == len(pieces) - 1
        out = grads(
            axes, scal, using, gate_pre, up_pre, gate_weight, up_weight, gate_m, up_m, acc, start, cols, last
        )
        acc = out[2]
        weights = weight_grads(x_t, out[0], out[1], gate_m, up_m, weights, gate_weight.shape, start)
    mine, theirs = out[2:-1], axes.to_core(out[-1])
    total = [m + theirs[s].astype(F32) for s, m in enumerate(mine)]
    run = None
    for s in list(range(1, axes.chips)) + [0]:
        run = total[s] if run is None else axes.to_next(run.astype(BF16)).astype(F32) + total[s]
    return (run.astype(BF16), weights[0], weights[1], grad_down)


def solution(mesh):
    in_specs = (
        P("tensor", "pipe"),
        P("tensor", "pipe"),
        P(None, "tensor"),
        P(None, "tensor"),
        P("pipe", "tensor"),
        P("pipe", "tensor"),
        P("tensor", "pipe"),
        P("pipe", "tensor"),
        P("pipe", "tensor"),
        P("tensor", "pipe"),
    )
    out_specs = (P("tensor", "pipe"), P("pipe", "tensor"), P("pipe", "tensor"), P("tensor", "pipe"))
    return jax.shard_map(
        functools.partial(shards, Axes(mesh)), mesh=mesh, in_specs=in_specs, out_specs=out_specs, check_vma=False
    )
```

```python
import functools

import jax
import jax.numpy as jnp
from jax import lax
from jax.experimental import pallas as pl
from jax.experimental.pallas import tpu as pltpu
from jax.sharding import PartitionSpec as P

BLOCK = 128
BF16 = jnp.bfloat16
F32 = jnp.float32
VMEM_BYTES = 60 * 1024 * 1024
NT = (((1,), (1,)), ((), ()))
NN = (((1,), (0,)), ((), ()))


def params():
    return pltpu.CompilerParams(vmem_limit_bytes=VMEM_BYTES)


def after(x, *others):
    return lax.optimization_barrier((x, *others))[0]


def step_of(hid):
    return 512 if hid % 512 == 0 else 256


def chunk_of(size, most):
    return max(c for c in (128, 256, 512, 1024) if size % c == 0 and c <= most)


def ring_of(chips):
    return [0] + list(range(1, chips, 2)) + [c for c in range(chips - 1, 0, -1) if c % 2 == 0]


class Axes:
    def __init__(self, mesh):
        self.tensor = mesh.shape["tensor"]
        self.chips = self.tensor // 2
        self.ring = ring_of(self.chips)

    def rows(self, tok):
        me = lax.axis_index("tensor")
        n = self.chips
        table = [[self.ring[(self.ring.index(c) - s) % n] for s in range(n)] for c in range(n)]
        chip = lax.dynamic_slice(jnp.array(table, jnp.int32), (me // 2, 0), (1, n))[0] * 2
        core = (me % 2).astype(jnp.int32)
        mine, other = (chip + core) * tok, (chip + 1 - core) * tok
        return jnp.concatenate([mine[:1], other[:1], mine[1:], other[1:]])

    def to_core(self, x):
        return lax.ppermute(x, "tensor", [(t, t ^ 1) for t in range(self.tensor)])

    def to_next(self, x):
        pairs = [(self.ring[i], self.ring[(i + 1) % self.chips]) for i in range(self.chips)]
        return lax.ppermute(x, "tensor", [(2 * a + k, 2 * b + k) for a, b in pairs for k in range(2)])


def partial_kernel(count, step, *refs):
    tokens = refs[:count]
    down, mask, out, rows = refs[count:]

    @pl.when(pl.program_id(0) == 0)
    def _():
        at = 0
        for ref in tokens:
            rows[at : at + ref.shape[0], :] = ref[...]
            at += ref.shape[0]

    kept = [down[i * BLOCK : (i + 1) * BLOCK, :] * mask[i].astype(BF16) for i in range(step // BLOCK)]
    acc = lax.dot_general(rows[...], jnp.concatenate(kept, axis=0), NT, preferred_element_type=F32)
    out[...] = acc.astype(BF16)


def partial_sums(tokens, down, mask, start, cols):
    width = down.shape[1]
    step = step_of(down.shape[0])
    rows = sum(t.shape[0] for t in tokens)
    first = start // step
    return pl.pallas_call(
        functools.partial(partial_kernel, len(tokens), step),
        out_shape=jax.ShapeDtypeStruct((rows, cols), BF16),
        grid=(cols // step,),
        in_specs=[pl.BlockSpec(t.shape, lambda k: (0, 0), pipeline_mode=pl.Buffered(1)) for t in tokens]
        + [
            pl.BlockSpec((step, width), lambda k: (first + k, 0)),
            pl.BlockSpec((step // BLOCK, 1, width), lambda k: (first + k, 0, 0)),
        ],
        out_specs=pl.BlockSpec((rows, step), lambda k: (0, k)),
        scratch_shapes=[pltpu.VMEM((rows, width), BF16)],
        compiler_params=params(),
        cost_estimate=pl.CostEstimate(
            flops=2 * rows * width * cols,
            bytes_accessed=2 * (rows * width + width * cols + rows * cols),
            transcendentals=0,
        ),
        name="partial_sums",
    )(*tokens, down, mask)


def grads_kernel(cfg, at_rows, *refs):
    refs = list(refs)
    take = lambda n: [refs.pop(0) for _ in range(n)]
    hidden = take(cfg["sources"])
    gate_pre, up_pre, gate_w, up_w, gate_m, up_m = take(6)
    acc_in = take(4) if cfg["acc_in"] else None
    gate_out, up_out, *acc = take(6)
    (both,) = refs
    step, tok = cfg["step"], cfg["tok"]
    k = pl.program_id(0)

    for i in range(cfg["groups"]):
        at = pl.ds(pl.multiple_of(at_rows[i], 16), tok)
        rows = slice(i * tok, (i + 1) * tok)
        lo = i * tok
        for ref in hidden:
            if lo < ref.shape[0]:
                break
            lo -= ref.shape[0]
        g = gate_pre[at, :].astype(F32)
        u = up_pre[at, :].astype(F32)
        h = ref[lo : lo + tok, :].astype(F32)
        sig = 1.0 / (1.0 + jnp.exp(-g))
        gg = (h * u * sig * (1.0 + g * (1.0 - sig))).astype(BF16)
        ug = (h * g * sig).astype(BF16)
        gate_out[rows, :] = gg
        up_out[rows, :] = ug
        both[rows, :step] = gg
        both[rows, step:] = ug

    chunk = cfg["chunk"]

    def tile(n, first):
        def masked(w, m):
            rows = []
            for i in range(chunk // BLOCK):
                at = pl.ds(pl.multiple_of(n * chunk + i * BLOCK, BLOCK), BLOCK)
                rows.append(w[at, :] * m[pl.ds(n * (chunk // BLOCK) + i, 1), :].astype(BF16))
            return jnp.concatenate(rows, axis=0)

        w = jnp.concatenate([masked(gate_w, gate_m), masked(up_w, up_m)], axis=1)
        to = pl.ds(pl.multiple_of(n * chunk, chunk), chunk)
        term = lax.dot_general(both[...], w, NT, preferred_element_type=F32)
        lo = 0
        for i, ref in enumerate(acc):
            part = term[lo : lo + ref.shape[0], :]
            lo += ref.shape[0]
            if not first:
                part += ref[:, to]
            elif acc_in is not None:
                part += acc_in[i][:, to]
            ref[:, to] = part

    tiles = cfg["width"] // chunk

    @pl.when(k == 0)
    def _():
        pl.loop(0, tiles)(lambda n: tile(n, True))

    @pl.when(k > 0)
    def _():
        pl.loop(0, tiles)(lambda n: tile(n, False))


def grads(at_rows, sources, gate_pre, up_pre, gate_w, up_w, gate_m, up_m, acc, tok, start, cols):
    tokens, hid = gate_pre.shape
    width = gate_w.shape[0]
    step = step_of(hid)
    first = start // step
    specs = [
        pl.BlockSpec((a.shape[0], step), lambda k, _, off=off // step: (0, off + k)) for a, off in sources
    ]
    col = lambda k, _: (0, first + k)
    one = lambda k, _: (0, 0)
    specs += [pl.BlockSpec((tokens, step), col)] * 2
    specs += [pl.BlockSpec((width, step), col)] * 2
    specs += [pl.BlockSpec((gate_m.shape[0], step), col)] * 2
    arrays = [a for a, _ in sources] + [gate_pre, up_pre, gate_w, up_w, gate_m, up_m]
    parts = [tok, tok, tokens // 2 - tok, tokens // 2 - tok]
    if acc is not None:
        specs += [pl.BlockSpec((n, width), one, pipeline_mode=pl.Buffered(1)) for n in parts]
        arrays += list(acc)
    cfg = dict(
        sources=len(sources), groups=tokens // tok, tok=tok, step=step, width=width, chunk=chunk_of(width, 1024),
        acc_in=acc is not None,
    )
    out = pl.pallas_call(
        functools.partial(grads_kernel, cfg),
        out_shape=[jax.ShapeDtypeStruct((tokens, cols), BF16)] * 2
        + [jax.ShapeDtypeStruct((n, width), F32) for n in parts],
        grid_spec=pltpu.PrefetchScalarGridSpec(
            num_scalar_prefetch=1,
            grid=(cols // step,),
            in_specs=specs,
            out_specs=[pl.BlockSpec((tokens, step), lambda k, _: (0, k))] * 2
            + [pl.BlockSpec((n, width), one) for n in parts],
            scratch_shapes=[pltpu.VMEM((tokens, 2 * step), BF16)],
        ),
        compiler_params=params(),
        cost_estimate=pl.CostEstimate(
            flops=4 * tokens * width * cols,
            bytes_accessed=4 * width * cols + 10 * tokens * cols + 8 * tokens * width,
            transcendentals=tokens * cols,
        ),
        name="hidden_grads",
    )(at_rows, *arrays)
    return out[0], out[1], out[2:]


def weights_kernel(cfg, x, gate, up, gate_m, up_m, *refs):
    outs = refs[-2:]
    chunk = cfg["chunk"]
    for g, m, out in ((gate, gate_m, outs[0]), (up, up_m, outs[1])):

        def tile(n, g=g, m=m, out=out):
            at = pl.ds(pl.multiple_of(n * chunk, chunk), chunk)
            term = lax.dot_general(x[at, :], g[...], NN, preferred_element_type=F32)
            for i in range(chunk // BLOCK):
                to = pl.ds(pl.multiple_of(n * chunk + i * BLOCK, BLOCK), BLOCK)
                row = m[pl.ds(n * (chunk // BLOCK) + i, 1), :]
                out[to, :] = (term[i * BLOCK : (i + 1) * BLOCK, :] * row).astype(BF16)

        pl.loop(0, cfg["width"] // chunk)(tile)


def weight_grads(x_t, gate, up, gate_m, up_m, before, shape, start):
    width, tokens = x_t.shape
    step = step_of(shape[1])
    steps = gate.shape[1] // step
    first = start // step
    col = lambda k: (0, first + k)
    specs = [
        pl.BlockSpec((width, tokens), lambda k: (0, 0), pipeline_mode=pl.Buffered(1)),
        pl.BlockSpec((tokens, step), lambda k: (0, k)),
        pl.BlockSpec((tokens, step), lambda k: (0, k)),
        pl.BlockSpec((gate_m.shape[0], step), col),
        pl.BlockSpec((gate_m.shape[0], step), col),
    ]
    arrays = [x_t, gate, up, gate_m, up_m]
    alias = {}
    if before is not None:
        specs += [pl.BlockSpec(memory_space=pl.ANY)] * 2
        arrays += list(before)
        alias = {5: 0, 6: 1}
    return pl.pallas_call(
        functools.partial(weights_kernel, dict(width=width, chunk=chunk_of(width, 1024))),
        out_shape=[jax.ShapeDtypeStruct(shape, BF16)] * 2,
        grid=(steps,),
        in_specs=specs,
        out_specs=[pl.BlockSpec((width, step), col)] * 2,
        input_output_aliases=alias,
        compiler_params=params(),
        cost_estimate=pl.CostEstimate(
            flops=4 * tokens * width * steps * step,
            bytes_accessed=4 * (width + tokens) * steps * step + 2 * tokens * width,
            transcendentals=0,
        ),
        name="weight_grads",
    )(*arrays)


def down_kernel(cfg, at_rows, *refs):
    tokens = refs[:4]
    gate_pre, up_pre, mask, out, rows, hidden = refs[4:]
    tok = cfg["tok"]

    @pl.when(pl.program_id(0) == 0)
    def _():
        at = 0
        for ref in tokens:
            rows[at : at + ref.shape[0], :] = ref[...]
            at += ref.shape[0]

    for i in range(cfg["groups"]):
        at = pl.ds(pl.multiple_of(at_rows[i], 16), tok)
        g = gate_pre[at, :].astype(F32)
        u = up_pre[at, :].astype(F32)
        hidden[i * tok : (i + 1) * tok, :] = (g * (1.0 / (1.0 + jnp.exp(-g))) * u).astype(BF16)
    across = hidden[...].T
    chunk = cfg["chunk"]

    def tile(n):
        at = pl.ds(pl.multiple_of(n * chunk, chunk), chunk)
        term = lax.dot_general(across, rows[:, at], NN, preferred_element_type=F32)
        for i in range(cfg["step"] // BLOCK):
            part = slice(i * BLOCK, (i + 1) * BLOCK)
            out[part, at] = (term[part, :] * mask[i, :, at]).astype(BF16)

    pl.loop(0, cfg["width"] // chunk)(tile)


def down_grad(at_rows, out_grad, gate_pre, up_pre, mask, tok):
    tokens, hid = gate_pre.shape
    width = out_grad[0].shape[1]
    step = step_of(hid)
    cfg = dict(groups=tokens // tok, tok=tok, width=width, step=step, chunk=chunk_of(width, 1024))
    return pl.pallas_call(
        functools.partial(down_kernel, cfg),
        out_shape=jax.ShapeDtypeStruct((hid, width), BF16),
        grid_spec=pltpu.PrefetchScalarGridSpec(
            num_scalar_prefetch=1,
            grid=(hid // step,),
            in_specs=[pl.BlockSpec(t.shape, lambda k, _: (0, 0), pipeline_mode=pl.Buffered(1)) for t in out_grad]
            + [pl.BlockSpec((tokens, step), lambda k, _: (0, k))] * 2
            + [pl.BlockSpec((step // BLOCK, 1, width), lambda k, _: (k, 0, 0))],
            out_specs=pl.BlockSpec((step, width), lambda k, _: (k, 0)),
            scratch_shapes=[pltpu.VMEM((tokens, width), BF16), pltpu.VMEM((tokens, step), BF16)],
        ),
        compiler_params=params(),
        cost_estimate=pl.CostEstimate(
            flops=2 * tokens * width * hid,
            bytes_accessed=2 * (tokens * width + 2 * tokens * hid + width * hid),
            transcendentals=tokens * hid,
        ),
        name="down_grad",
    )(at_rows, *out_grad, gate_pre, up_pre, mask)


def round_ring(axes, x):
    got = [x]
    for _ in range(axes.chips - 1):
        got.append(axes.to_next(got[-1]))
    return jnp.concatenate(got[1:], axis=0)


def shards(axes, layer_input, out_grad, gate_pre, up_pre, gate_weight, up_weight, down_weight, gate_mask, up_mask, down_mask):
    tokens, hid = gate_pre.shape
    tok = out_grad.shape[0]
    step = step_of(hid)
    at_rows = axes.rows(tok)
    gate_m = jnp.repeat(gate_mask, BLOCK, axis=1).astype(F32)
    up_m = jnp.repeat(up_mask, BLOCK, axis=1).astype(F32)
    down_m = jnp.repeat(down_mask, BLOCK, axis=1).astype(F32)[:, None, :]

    near = [out_grad, axes.to_core(out_grad)]
    early = lax.psum(partial_sums(near, down_weight, down_m, 0, hid), "pipe")
    far = round_ring(axes, out_grad)
    far = [far, axes.to_core(far)]
    x_far = round_ring(axes, after(layer_input, far[0]))
    x_other = axes.to_core(jnp.concatenate([layer_input, x_far], axis=0))

    pieces, at = [], 0
    while at < hid:
        pieces.append((at, min(2 * step, hid - at)))
        at += pieces[-1][1]
    parts = [partial_sums(far, down_weight, down_m, start, cols) for start, cols in pieces]
    late, last = [], early
    for p in parts:
        last = lax.psum(after(p, last), "pipe")
        late.append(last)
    grad_down = down_grad(after(at_rows, *parts), near + far, gate_pre, up_pre, down_m, tok)
    x_t = jnp.concatenate([layer_input, x_other[:tok], x_far, x_other[tok:]], axis=0).T

    acc, weights = None, None
    at_rows = after(at_rows, grad_down, x_t)
    for i, ((start, cols), hidden) in enumerate(zip(pieces, late)):
        if i >= 1 and i < len(pieces) - 1:
            at_rows, *weights = lax.optimization_barrier((at_rows, *weights))
        gate, up, acc = grads(
            at_rows, [(early, start), (hidden, 0)], gate_pre, up_pre, gate_weight, up_weight, gate_m, up_m, acc, tok,
            start, cols,
        )
        weights = weight_grads(x_t, gate, up, gate_m, up_m, weights, gate_weight.shape, start)
    mine, other, mine_far, other_far = acc
    far = mine_far + axes.to_core(other_far)
    near = mine + axes.to_core(other)
    run = far[:tok]
    for s in range(1, axes.chips):
        term = far[s * tok : (s + 1) * tok] if s < axes.chips - 1 else near
        run = axes.to_next(run.astype(BF16)).astype(F32) + term
    return (run.astype(BF16), weights[0], weights[1], grad_down)


def solution(mesh):
    in_specs = (
        P("tensor", "pipe"),
        P("tensor", "pipe"),
        P(None, "tensor"),
        P(None, "tensor"),
        P("pipe", "tensor"),
        P("pipe", "tensor"),
        P("tensor", "pipe"),
        P("pipe", "tensor"),
        P("pipe", "tensor"),
        P("tensor", "pipe"),
    )
    out_specs = (P("tensor", "pipe"), P("pipe", "tensor"), P("pipe", "tensor"), P("tensor", "pipe"))
    return jax.shard_map(
        functools.partial(shards, Axes(mesh)), mesh=mesh, in_specs=in_specs, out_specs=out_specs, check_vma=False
    )
```

```python
import functools
import math

import jax
import jax.numpy as jnp
from jax import lax
from jax.experimental import pallas as pl
from jax.experimental.pallas import tpu as pltpu
from jax.sharding import PartitionSpec as P

BLOCK = 128
BF16 = jnp.bfloat16
F32 = jnp.float32
VMEM_BYTES = 60 * 1024 * 1024
NT = (((1,), (1,)), ((), ()))
NN = (((1,), (0,)), ((), ()))


def params():
    return pltpu.CompilerParams(vmem_limit_bytes=VMEM_BYTES)


def after(x, *others):
    return lax.optimization_barrier((x, *others))[0]


def step_of(hid):
    return 512 if hid % 512 == 0 else 256


def chunk_of(size, most):
    return max(c for c in (128, 256, 512, 1024) if size % c == 0 and c <= most)


def ring_of(chips):
    return [0] + list(range(1, chips, 2)) + [c for c in range(chips - 1, 0, -1) if c % 2 == 0]


class Axes:
    def __init__(self, mesh):
        self.pipe = mesh.shape["pipe"]
        self.tensor = mesh.shape["tensor"]
        self.chips = self.tensor // 2
        self.ring = ring_of(self.chips)

    def slots(self):
        n = self.chips
        table = [[self.ring[(self.ring.index(c) - s) % n] for s in range(n)] for c in range(n)]
        return lax.dynamic_slice(jnp.array(table, jnp.int32), (lax.axis_index("tensor") // 2, 0), (1, n))[0]

    def rows(self, tok):
        chip = self.slots() * 2
        core = (lax.axis_index("tensor") % 2).astype(jnp.int32)
        mine, other = (chip + core) * tok, (chip + 1 - core) * tok
        place = lax.axis_index("pipe").astype(jnp.int32).reshape(1)
        return jnp.concatenate([mine[:1], other[:1], mine[1:], other[1:], place])

    def to_core(self, x):
        return lax.ppermute(x, "tensor", [(t, t ^ 1) for t in range(self.tensor)])

    def to_pipe(self, x, bit):
        return lax.ppermute(x, "pipe", [(i, i ^ bit) for i in range(self.pipe)])

    def to_next(self, x):
        pairs = [(self.ring[i], self.ring[(i + 1) % self.chips]) for i in range(self.chips)]
        return lax.ppermute(x, "tensor", [(2 * a + k, 2 * b + k) for a, b in pairs for k in range(2)])


def reduce_over_pipe(axes, partial, order):
    place = lax.axis_index("pipe")
    bits = axes.pipe.bit_length() - 1
    rows, cols = partial.shape
    left = partial.reshape((2,) * bits + (rows // axes.pipe, cols))
    for bit in order:
        axis = bits - bit.bit_length()
        here = (place // bit) % 2
        send = lax.dynamic_slice_in_dim(left, 1 - here, 1, axis).astype(BF16)
        keep = lax.dynamic_slice_in_dim(left, here, 1, axis)
        left = keep + axes.to_pipe(send, bit).astype(F32)
    held = {0: left.reshape(rows // axes.pipe, cols).astype(BF16)}
    for bit in reversed(order):
        for r in list(held):
            held[r ^ bit] = axes.to_pipe(held[r], bit)
    return [held[r] for r in range(axes.pipe)]


def grads_kernel(cfg, at_rows, *refs):
    refs = list(refs)
    sources = [[refs.pop(0) for _ in range(cfg["pipe"])] for _ in cfg["sources"]]
    gate_pre, up_pre, gate_out, up_out, hidden = refs
    k = pl.program_id(0)
    place = at_rows[cfg["groups"]]
    tok = cfg["tok"]

    for src, arrays in zip(cfg["sources"], sources):

        def copy(src=src, arrays=arrays):
            for r in range(cfg["pipe"]):
                to = src["base"] + (place ^ r) * src["part"]
                hidden[pl.ds(pl.multiple_of(to, 16), src["part"]), :] = arrays[r][...]

        if src["lo"] <= 0 and src["hi"] >= cfg["steps"]:
            copy()
        else:
            pl.when((k >= src["lo"]) & (k < src["hi"]))(copy)

    for i in range(cfg["groups"]):
        at = pl.ds(pl.multiple_of(at_rows[i], 16), tok)
        g = gate_pre[at, :].astype(F32)
        u = up_pre[at, :].astype(F32)
        h = hidden[i * tok : (i + 1) * tok, :].astype(F32)
        sig = 1.0 / (1.0 + jnp.exp(-g))
        gate_out[at, :] = (h * u * sig * (1.0 + g * (1.0 - sig))).astype(BF16)
        up_out[at, :] = (h * g * sig).astype(BF16)


def local_grads(axes, at_rows, sources, gate_pre, up_pre, tok, start, cols):
    tokens = gate_pre.shape[0]
    step = start
    for _, _, c0, w in sources:
        step = math.gcd(step, math.gcd(c0, w))
    step = step or cols
    first = start // step
    infos, specs, arrays = [], [], []
    for parts, base, c0, w in sources:
        part = parts[0].shape[0]
        lo, n = (c0 - start) // step, w // step
        infos.append(dict(base=base, part=part, lo=lo, hi=lo + n))
        arrays += parts
        spec = pl.BlockSpec((part, step), lambda k, _, lo=lo, n=n: (0, jnp.clip(k - lo, 0, n - 1)))
        specs += [spec] * len(parts)
    specs += [pl.BlockSpec((tokens, step), lambda k, _: (0, first + k))] * 2
    cfg = dict(sources=infos, pipe=axes.pipe, groups=tokens // tok, tok=tok, steps=cols // step)
    return pl.pallas_call(
        functools.partial(grads_kernel, cfg),
        out_shape=[jax.ShapeDtypeStruct((tokens, cols), BF16)] * 2,
        grid_spec=pltpu.PrefetchScalarGridSpec(
            num_scalar_prefetch=1,
            grid=(cols // step,),
            in_specs=specs,
            out_specs=[pl.BlockSpec((tokens, step), lambda k, _: (0, k))] * 2,
            scratch_shapes=[pltpu.VMEM((tokens, step), BF16)],
        ),
        compiler_params=params(),
        cost_estimate=pl.CostEstimate(
            flops=20 * tokens * cols, bytes_accessed=10 * tokens * cols, transcendentals=2 * tokens * cols
        ),
        name="local_grads",
    )(at_rows, *arrays, gate_pre, up_pre)


def down_kernel(cfg, at_rows, *refs):
    tokens = refs[:4]
    gate_pre, up_pre, mask, out, rows, hidden = refs[4:]
    tok = cfg["tok"]

    @pl.when(pl.program_id(0) == 0)
    def _():
        at = 0
        for ref in tokens:
            rows[at : at + ref.shape[0], :] = ref[...]
            at += ref.shape[0]

    for i in range(cfg["groups"]):
        at = pl.ds(pl.multiple_of(at_rows[i], 16), tok)
        g = gate_pre[at, :].astype(F32)
        u = up_pre[at, :].astype(F32)
        hidden[i * tok : (i + 1) * tok, :] = (g * (1.0 / (1.0 + jnp.exp(-g))) * u).astype(BF16)
    across = hidden[...].T
    chunk = cfg["chunk"]

    def tile(n):
        at = pl.ds(pl.multiple_of(n * chunk, chunk), chunk)
        term = lax.dot_general(across, rows[:, at], NN, preferred_element_type=F32)
        for i in range(cfg["step"] // BLOCK):
            part = slice(i * BLOCK, (i + 1) * BLOCK)
            out[part, at] = (term[part, :] * mask[i, :, at]).astype(BF16)

    pl.loop(0, cfg["width"] // chunk)(tile)


def down_grad(at_rows, out_grad, gate_pre, up_pre, mask, tok):
    tokens, hid = gate_pre.shape
    width = out_grad[0].shape[1]
    step = step_of(hid)
    cfg = dict(groups=tokens // tok, tok=tok, width=width, step=step, chunk=chunk_of(width, 1024))
    return pl.pallas_call(
        functools.partial(down_kernel, cfg),
        out_shape=jax.ShapeDtypeStruct((hid, width), BF16),
        grid_spec=pltpu.PrefetchScalarGridSpec(
            num_scalar_prefetch=1,
            grid=(hid // step,),
            in_specs=[pl.BlockSpec(t.shape, lambda k, _: (0, 0), pipeline_mode=pl.Buffered(1)) for t in out_grad]
            + [pl.BlockSpec((tokens, step), lambda k, _: (0, k))] * 2
            + [pl.BlockSpec((step // BLOCK, 1, width), lambda k, _: (k, 0, 0))],
            out_specs=pl.BlockSpec((step, width), lambda k, _: (k, 0)),
            scratch_shapes=[pltpu.VMEM((tokens, width), BF16), pltpu.VMEM((tokens, step), BF16)],
        ),
        compiler_params=params(),
        cost_estimate=pl.CostEstimate(
            flops=2 * tokens * width * hid,
            bytes_accessed=2 * (tokens * width + 2 * tokens * hid + width * hid),
            transcendentals=tokens * hid,
        ),
        name="down_grad",
    )(at_rows, *out_grad, gate_pre, up_pre, mask)


def masked(weight, mask):
    rows, cols = weight.shape
    return (weight.reshape(rows // BLOCK, BLOCK, cols) * mask.astype(BF16)[:, None, :]).reshape(rows, cols)


def round_ring(axes, x):
    half = x.shape[0] // 2
    now = [x[:half], x[half:]]
    got = []
    for _ in range(axes.chips - 1):
        now = [axes.to_next(a) for a in now]
        got += now
    return jnp.concatenate(got, axis=0)


def halves(start, cols):
    first = cols // 2 if cols // 2 % BLOCK == 0 else cols // 2 // BLOCK * BLOCK + BLOCK
    return [(start, first), (start + first, cols - first)]


def dot_nt(a, b):
    return lax.dot_general(a, b, NT, preferred_element_type=F32)


def weight_grad(x, grad, mask):
    tokens, width = x.shape
    blocks = width // BLOCK
    out = lax.dot_general(
        x.reshape(tokens, blocks, BLOCK), grad, (((0,), (0,)), ((), ())), preferred_element_type=F32
    )
    return (out * mask[:, None, :]).astype(BF16).reshape(width, grad.shape[1])


def shards(axes, layer_input, out_grad, gate_pre, up_pre, gate_weight, up_weight, down_weight, gate_mask, up_mask, down_mask):
    tokens, hid = gate_pre.shape
    tok, width = out_grad.shape
    at_rows = axes.rows(tok)
    gate_m = jnp.repeat(gate_mask, BLOCK, axis=1).astype(F32)
    up_m = jnp.repeat(up_mask, BLOCK, axis=1).astype(F32)
    down_m = jnp.repeat(down_mask, BLOCK, axis=1).astype(F32)
    bits = [1 << i for i in range(axes.pipe.bit_length() - 1)]
    orders = [bits, bits[::-1]]
    pieces = halves(0, hid)

    near = [out_grad, axes.to_core(out_grad)]
    far = round_ring(axes, out_grad)
    far = [far, axes.to_core(far)]

    downs = [masked(down_weight[c : c + w], down_m[c // BLOCK : (c + w) // BLOCK]) for c, w in pieces]
    near_rows = jnp.concatenate(near, axis=0)
    split_near = 2 * tok % (16 * axes.pipe) == 0
    sources = [[] for _ in pieces]
    if split_near:
        for j, (c, w) in enumerate(pieces):
            total = reduce_over_pipe(axes, dot_nt(near_rows, downs[j]), orders[j])
            sources[j].append((total, 0, c, w))
    gates = [masked(gate_weight[:, c : c + w], gate_m[:, c : c + w]) for c, w in pieces]
    ups = [masked(up_weight[:, c : c + w], up_m[:, c : c + w]) for c, w in pieces]
    far_rows = after(jnp.concatenate(far, axis=0), *gates, *ups)
    if not split_near:
        far_rows = jnp.concatenate([near_rows, far_rows], axis=0)
    parts = []
    for j, (c, w) in enumerate(pieces):
        parts.append(dot_nt(far_rows, downs[j]))
        for order, (sc, sw) in zip(orders, halves(c, w)):
            total = reduce_over_pipe(axes, parts[j][:, sc - c : sc - c + sw], order)
            sources[j].append((total, 2 * tok if split_near else 0, sc, sw))

    x = lax.all_gather(after(layer_input, far_rows), "tensor", axis=0, tiled=True)
    grad_down = down_grad(after(at_rows, *parts), near + far, gate_pre, up_pre, down_m[:, None, :], tok)
    at_rows = after(at_rows, grad_down)

    acc, gate_grads, up_grads = None, [], []
    for j, (c, w) in enumerate(pieces):
        gate, up = local_grads(axes, at_rows, sources[j], gate_pre, up_pre, tok, c, w)
        term = dot_nt(gate, gates[j]) + dot_nt(up, ups[j])
        acc = term if acc is None else acc + term
        gate_grads.append(gate)
        up_grads.append(up)

    core = lax.axis_index("tensor") % 2
    slots = axes.slots()
    by_core = acc.reshape(axes.chips, 2, tok, width)
    pick = lambda a, i, axis: lax.dynamic_index_in_dim(a, i, axis, keepdims=False)
    total = pick(by_core, core, 1) + axes.to_core(pick(by_core, 1 - core, 1))
    grad_input = []
    for i in range(2):
        half = total[:, :, i * (width // 2) : (i + 1) * (width // 2)]
        run = pick(half, slots[1 % axes.chips], 0)
        for s in range(1, axes.chips):
            run = axes.to_next(run.astype(BF16)).astype(F32) + pick(half, slots[(s + 1) % axes.chips], 0)
        grad_input.append(run.astype(BF16))
    grad_gate = weight_grad(x, jnp.concatenate(gate_grads, axis=1), gate_m)
    grad_up = weight_grad(x, jnp.concatenate(up_grads, axis=1), up_m)
    return (jnp.concatenate(grad_input, axis=1), grad_gate, grad_up, grad_down)


def solution(mesh):
    in_specs = (
        P("tensor", "pipe"),
        P("tensor", "pipe"),
        P(None, "tensor"),
        P(None, "tensor"),
        P("pipe", "tensor"),
        P("pipe", "tensor"),
        P("tensor", "pipe"),
        P("pipe", "tensor"),
        P("pipe", "tensor"),
        P("tensor", "pipe"),
    )
    out_specs = (P("tensor", "pipe"), P("pipe", "tensor"), P("pipe", "tensor"), P("tensor", "pipe"))
    return jax.shard_map(
        functools.partial(shards, Axes(mesh)), mesh=mesh, in_specs=in_specs, out_specs=out_specs, check_vma=False
    )
```

```python
import functools

import jax
import jax.numpy as jnp
from jax import lax
from jax.experimental import pallas as pl
from jax.experimental.pallas import tpu as pltpu
from jax.sharding import PartitionSpec as P

BLOCK = 128
BF16 = jnp.bfloat16
F32 = jnp.float32
VMEM_BYTES = 60 * 1024 * 1024
NT = (((1,), (1,)), ((), ()))
NN = (((1,), (0,)), ((), ()))


def params():
    return pltpu.CompilerParams(vmem_limit_bytes=VMEM_BYTES)


def after(x, *others):
    return lax.optimization_barrier((x, *others))[0]


def step_of(hid):
    return 512 if hid % 512 == 0 else 256


def chunk_of(size, most):
    return max(c for c in (128, 256, 512, 1024) if size % c == 0 and c <= most)


def ring_of(chips):
    return [0] + list(range(1, chips, 2)) + [c for c in range(chips - 1, 0, -1) if c % 2 == 0]


class Axes:
    def __init__(self, mesh):
        self.pipe = mesh.shape["pipe"]
        self.tensor = mesh.shape["tensor"]
        self.chips = self.tensor // 2
        self.ring = ring_of(self.chips)

    def slots(self):
        n = self.chips
        table = [[self.ring[(self.ring.index(c) - s) % n] for s in range(n)] for c in range(n)]
        return lax.dynamic_slice(jnp.array(table, jnp.int32), (lax.axis_index("tensor") // 2, 0), (1, n))[0]

    def rows(self, tok):
        chip = self.slots() * 2
        core = (lax.axis_index("tensor") % 2).astype(jnp.int32)
        mine, other = (chip + core) * tok, (chip + 1 - core) * tok
        place = lax.axis_index("pipe").astype(jnp.int32).reshape(1)
        return jnp.concatenate([mine[:1], other[:1], mine[1:], other[1:], place])

    def to_core(self, x):
        return lax.ppermute(x, "tensor", [(t, t ^ 1) for t in range(self.tensor)])

    def to_pipe(self, x, bit):
        return lax.ppermute(x, "pipe", [(i, i ^ bit) for i in range(self.pipe)])

    def to_next(self, x):
        pairs = [(self.ring[i], self.ring[(i + 1) % self.chips]) for i in range(self.chips)]
        return lax.ppermute(x, "tensor", [(2 * a + k, 2 * b + k) for a, b in pairs for k in range(2)])


def reduce_over_pipe(axes, partial):
    place = lax.axis_index("pipe")
    bits = axes.pipe.bit_length() - 1
    rows, cols = partial.shape
    left = partial.reshape((2,) * bits + (rows // axes.pipe, cols))
    for i in range(bits):
        axis = bits - 1 - i
        here = (place >> i) % 2
        send = lax.dynamic_slice_in_dim(left, 1 - here, 1, axis).astype(BF16)
        keep = lax.dynamic_slice_in_dim(left, here, 1, axis)
        left = keep + axes.to_pipe(send, 1 << i).astype(F32)
    held = {0: left.reshape(rows // axes.pipe, cols).astype(BF16)}
    for i in reversed(range(bits)):
        for r in list(held):
            held[r ^ (1 << i)] = axes.to_pipe(held[r], 1 << i)
    return [(held[r], r, 0) for r in range(axes.pipe)]


class Square:
    def __init__(self, axes, partial):
        self.axes, self.partial = axes, partial
        self.part = partial.shape[0] // 4
        self.half = self.part // 2

    def block(self, r, first, count):
        at = ((lax.axis_index("pipe") ^ r) * self.part + first, 0)
        return lax.dynamic_slice(self.partial, at, (count, self.partial.shape[1]))

    def send(self, for_1, for_2, others):
        for_1, for_2 = lax.optimization_barrier((for_1, for_2, *others))[:2] if others else (for_1, for_2)
        return self.axes.to_pipe(for_1, 1), self.axes.to_pipe(for_2, 2)

    def corner(self, others):
        half = self.half
        self.by = self.send(self.block(3, 0, half).astype(BF16), self.block(3, half, half).astype(BF16), others)

    def sides(self, others):
        half = self.half
        by_1, by_2 = [a.astype(F32) for a in self.by]
        for_1 = jnp.concatenate([self.block(1, 0, half), self.block(1, half, half) + by_2], axis=0).astype(BF16)
        for_2 = jnp.concatenate([self.block(2, 0, half) + by_1, self.block(2, half, half)], axis=0).astype(BF16)
        self.terms = self.send(for_1, for_2, others)

    def back(self, others, zero=0.0):
        mine = self.block(0, 0, self.part) + self.terms[0].astype(F32) + self.terms[1].astype(F32)
        self.mine = (mine + zero).astype(BF16)
        self.near = self.send(self.mine, self.mine, others)

    def across(self, others, zero=0.0):
        for_1, for_2 = self.near[1][self.half :], self.near[0][: self.half]
        self.far = self.send(for_1 + jnp.asarray(zero, BF16), for_2 + jnp.asarray(zero, BF16), others)

    def result(self):
        return [
            (self.mine, 0, 0),
            (self.near[0], 1, 0),
            (self.near[1], 2, 0),
            (self.far[1], 3, 0),
            (self.far[0], 3, self.half),
        ]


def mask_kernel(gate, up, gate_m, up_m, out):
    for j, (w, m) in enumerate(((gate, gate_m), (up, up_m))):

        @pl.when(pl.program_id(0) == j)
        def _(w=w, m=m):
            for i in range(out.shape[0] // BLOCK):
                rows = slice(i * BLOCK, (i + 1) * BLOCK)
                out[rows, :] = w[rows, :] * m[i : i + 1, :].astype(BF16)


def masked_pair(gate, up, gate_m, up_m, start, cols, step):
    width = gate.shape[0]
    first, steps = start // step, cols // step
    one = lambda j, k: (0, first + jnp.where(j == 0, k, steps - 1))
    two = lambda j, k: (0, first + jnp.where(j == 0, 0, k))
    return pl.pallas_call(
        mask_kernel,
        out_shape=jax.ShapeDtypeStruct((width, 2 * cols), BF16),
        grid=(2, steps),
        in_specs=[pl.BlockSpec((a.shape[0], step), i) for a, i in ((gate, one), (up, two), (gate_m, one), (up_m, two))],
        out_specs=pl.BlockSpec((width, step), lambda j, k: (0, j * steps + k)),
        compiler_params=params(),
        cost_estimate=pl.CostEstimate(flops=2 * width * cols, bytes_accessed=8 * width * cols, transcendentals=0),
        name="masked_pair",
    )(gate, up, gate_m, up_m)


def sigmoid(g):
    return 0.5 + 0.5 * jnp.tanh(0.5 * g)


def grads_kernel(cfg, at_rows, *refs):
    count = len(cfg["sources"])
    parts = refs[:count]
    gate_pre, up_pre, out, gate_out, up_out, hidden = refs[count:]
    place = at_rows[cfg["groups"]]
    tok = cfg["tok"]

    @pl.when(pl.program_id(1) == 0)
    def _():
        for (r, first), ref in zip(cfg["sources"], parts):
            to = (place ^ r) * cfg["part"] + first
            hidden[pl.ds(pl.multiple_of(to, 16), ref.shape[0]), :] = ref[...]
        for i in range(cfg["groups"]):
            at = pl.ds(pl.multiple_of(at_rows[i], 16), tok)
            g = gate_pre[at, :].astype(F32)
            u = up_pre[at, :].astype(F32)
            h = hidden[i * tok : (i + 1) * tok, :].astype(F32)
            sig = sigmoid(g)
            h = h * sig
            gate = (h * u * (1.0 + g * (1.0 - sig))).astype(BF16)
            out[at, :] = gate
            gate_out[at, :] = gate
            up_out[at, :] = (h * g).astype(BF16)

    @pl.when(pl.program_id(1) == 1)
    def _():
        out[...] = up_out[...]


def local_grads(axes, at_rows, sources, gate_pre, up_pre, tok, start, cols, step):
    tokens = gate_pre.shape[0]
    first, steps = start // step, cols // step
    specs = [pl.BlockSpec((a.shape[0], step), lambda k, j, _: (0, k)) for a, _, _ in sources]
    specs += [pl.BlockSpec((tokens, step), lambda k, j, _: (0, first + k))] * 2
    cfg = dict(sources=[(r, lo) for _, r, lo in sources], part=tokens // axes.pipe, groups=tokens // tok, tok=tok)
    return pl.pallas_call(
        functools.partial(grads_kernel, cfg),
        out_shape=[jax.ShapeDtypeStruct((tokens, n * cols), BF16) for n in (2, 1, 1)],
        grid_spec=pltpu.PrefetchScalarGridSpec(
            num_scalar_prefetch=1,
            grid=(steps, 2),
            in_specs=specs,
            out_specs=[pl.BlockSpec((tokens, step), lambda k, j, _: (0, j * steps + k))]
            + [pl.BlockSpec((tokens, step), lambda k, j, _: (0, k))] * 2,
            scratch_shapes=[pltpu.VMEM((tokens, step), BF16)],
        ),
        compiler_params=params(),
        cost_estimate=pl.CostEstimate(
            flops=20 * tokens * cols, bytes_accessed=10 * tokens * cols, transcendentals=2 * tokens * cols
        ),
        name="local_grads",
    )(at_rows, *[a for a, _, _ in sources], gate_pre, up_pre)


def down_kernel(cfg, at_rows, *refs):
    tokens = refs[:4]
    gate_pre, up_pre, mask = refs[4:7]
    out, done, rows, hidden = refs[-4:]
    tok = cfg["tok"]

    @pl.when(pl.program_id(0) == 0)
    def _():
        done[...] = jnp.zeros_like(done)
        at = 0
        for ref in tokens:
            rows[at : at + ref.shape[0], :] = ref[...]
            at += ref.shape[0]

    for i in range(cfg["groups"]):
        at = pl.ds(pl.multiple_of(at_rows[i], 16), tok)
        g = gate_pre[at, :].astype(F32)
        u = up_pre[at, :].astype(F32)
        hidden[i * tok : (i + 1) * tok, :] = (g * sigmoid(g) * u).astype(BF16)
    across = hidden[...].T
    chunk = cfg["chunk"]

    def tile(n):
        at = pl.ds(pl.multiple_of(n * chunk, chunk), chunk)
        term = lax.dot_general(across, rows[:, at], NN, preferred_element_type=F32)
        for i in range(cfg["step"] // BLOCK):
            part = slice(i * BLOCK, (i + 1) * BLOCK)
            out[part, at] = (term[part, :] * mask[i, :, at]).astype(BF16)

    pl.loop(0, cfg["width"] // chunk)(tile)


def down_grad(at_rows, out_grad, gate_pre, up_pre, mask, tok, before, first, last):
    tokens, hid = gate_pre.shape
    width = out_grad[0].shape[1]
    step = step_of(hid)
    cfg = dict(groups=tokens // tok, tok=tok, width=width, step=step, chunk=chunk_of(width, 1024))
    specs = [pl.BlockSpec(t.shape, lambda k, _: (0, 0), pipeline_mode=pl.Buffered(1)) for t in out_grad]
    specs += [pl.BlockSpec((tokens, step), lambda k, _: (0, first + k))] * 2
    specs += [pl.BlockSpec((step // BLOCK, 1, width), lambda k, _: (first + k, 0, 0))]
    arrays = [*out_grad, gate_pre, up_pre, mask]
    alias = {}
    if before is not None:
        specs.append(pl.BlockSpec(memory_space=pl.ANY))
        arrays.append(before)
        alias = {len(arrays): 0}
    cols = (last - first) * step
    return pl.pallas_call(
        functools.partial(down_kernel, cfg),
        out_shape=[jax.ShapeDtypeStruct((hid, width), BF16), jax.ShapeDtypeStruct((8, 128), F32)],
        grid_spec=pltpu.PrefetchScalarGridSpec(
            num_scalar_prefetch=1,
            grid=(last - first,),
            in_specs=specs,
            out_specs=[
                pl.BlockSpec((step, width), lambda k, _: (first + k, 0)),
                pl.BlockSpec((8, 128), lambda k, _: (0, 0)),
            ],
            scratch_shapes=[pltpu.VMEM((tokens, width), BF16), pltpu.VMEM((tokens, step), BF16)],
        ),
        input_output_aliases=alias,
        compiler_params=params(),
        cost_estimate=pl.CostEstimate(
            flops=2 * tokens * width * cols,
            bytes_accessed=2 * (tokens * width + 2 * tokens * cols + width * cols),
            transcendentals=tokens * cols,
        ),
        name="down_grad",
    )(at_rows, *arrays)


def masked(weight, mask):
    rows, cols = weight.shape
    return (weight.reshape(rows // BLOCK, BLOCK, cols) * mask.astype(BF16)[:, None, :]).reshape(rows, cols)


def dot_nt(a, b):
    return lax.dot_general(a, b, NT, preferred_element_type=F32)


def weight_grad(x, grad, mask):
    tokens, width = x.shape
    blocks = width // BLOCK
    out = lax.dot_general(
        x.reshape(tokens, blocks, BLOCK), grad, (((0,), (0,)), ((), ())), preferred_element_type=F32
    )
    return (out * mask[:, None, :]).astype(BF16).reshape(width, grad.shape[1])


def shards(axes, layer_input, out_grad, gate_pre, up_pre, gate_weight, up_weight, down_weight, gate_mask, up_mask, down_mask):
    tokens, hid = gate_pre.shape
    tok, width = out_grad.shape
    blocks = hid // BLOCK
    third = (blocks + 2) // 3 * BLOCK
    pieces = [(0, third), (third, third), (2 * third, hid - 2 * third)]
    step = 256 if third % 256 == 0 and hid % 256 == 0 else BLOCK
    at_rows = axes.rows(tok)
    gate_m = jnp.repeat(gate_mask, BLOCK, axis=1).astype(F32)
    up_m = jnp.repeat(up_mask, BLOCK, axis=1).astype(F32)
    down_m = jnp.repeat(down_mask, BLOCK, axis=1).astype(F32)

    near = [out_grad, axes.to_core(out_grad)]
    downs = [masked(down_weight[c : c + w], down_m[c // BLOCK : (c + w) // BLOCK]) for c, w in pieces]
    pairs = []
    half = tok // 2
    now, got = [out_grad[:half], out_grad[half:]], []
    for s in range(axes.chips - 1):
        if s and s <= len(pieces):
            now = lax.optimization_barrier((*now, pairs[s - 1]))[:2]
        now = [axes.to_next(a) for a in now]
        if s < len(pieces):
            c, w = pieces[s]
            m = after(gate_m, *got[-2:])
            pairs.append(masked_pair(gate_weight, up_weight, m, up_m, c, w, step))
        got += now
    for c, w in pieces[len(pairs) :]:
        pairs.append(masked_pair(gate_weight, up_weight, gate_m, up_m, c, w, step))
    far = jnp.concatenate(got, axis=0)
    far = [far, axes.to_core(far)]
    rows = after(jnp.concatenate(near + far, axis=0), *pairs)

    parts = [dot_nt(rows, d) for d in downs]
    x = lax.all_gather(after(layer_input, rows), "tensor", axis=0, tiled=True)
    down = functools.partial(down_grad, out_grad=near + far, gate_pre=gate_pre, up_pre=up_pre, mask=down_m[:, None, :], tok=tok)
    steps = hid // step_of(hid)
    if axes.pipe == 4:
        squares = [Square(axes, p) for p in parts]
        for i, sq in enumerate(squares):
            prev = squares[i - 1] if i else None
            sq.corner(prev.by if i else [])
            if not i:
                grad_down, done = down(after(at_rows, *sq.by), before=None, first=0, last=(steps + 1) // 2)
            sq.sides(prev.terms if i else [])
            sq.back(prev.near if i else [], 0.0 if i else done[0, 0])
            if not i:
                grad_down, done = down(after(at_rows, *sq.terms), before=grad_down, first=(steps + 1) // 2, last=steps)
            sq.across(prev.far if i else [], 0.0 if i else done[0, 0])
        sums = [sq.result() for sq in squares]
    else:
        sums = [reduce_over_pipe(axes, p) for p in parts]
        grad_down, _ = down(after(at_rows, *parts), before=None, first=0, last=steps)
    at_rows = at_rows + (x[0, 0].astype(F32) * 0.0).astype(jnp.int32)

    acc, gate_grads, up_grads = None, [], []
    for (c, w), sources, pair in zip(pieces, sums, pairs):
        both, gate, up = local_grads(axes, at_rows, sources, gate_pre, up_pre, tok, c, w, step)
        term = dot_nt(both, pair)
        acc = term if acc is None else acc + term
        acc, at_rows = lax.optimization_barrier((acc, at_rows))
        gate_grads.append(gate)
        up_grads.append(up)

    core = lax.axis_index("tensor") % 2
    slots = axes.slots()
    by_core = acc.reshape(axes.chips, 2, tok, width)
    pick = lambda a, i, axis: lax.dynamic_index_in_dim(a, i, axis, keepdims=False)
    total = pick(by_core, core, 1) + axes.to_core(pick(by_core, 1 - core, 1))
    grad_input = []
    for i in range(2):
        half = total[:, :, i * (width // 2) : (i + 1) * (width // 2)]
        run = pick(half, slots[1 % axes.chips], 0)
        for s in range(1, axes.chips):
            run = axes.to_next(run.astype(BF16)).astype(F32) + pick(half, slots[(s + 1) % axes.chips], 0)
        grad_input.append(run.astype(BF16))
    grad_gate = weight_grad(x, jnp.concatenate(gate_grads, axis=1), gate_m)
    grad_up = weight_grad(x, jnp.concatenate(up_grads, axis=1), up_m)
    return (jnp.concatenate(grad_input, axis=1), grad_gate, grad_up, grad_down)


def solution(mesh):
    in_specs = (
        P("tensor", "pipe"),
        P("tensor", "pipe"),
        P(None, "tensor"),
        P(None, "tensor"),
        P("pipe", "tensor"),
        P("pipe", "tensor"),
        P("tensor", "pipe"),
        P("pipe", "tensor"),
        P("pipe", "tensor"),
        P("tensor", "pipe"),
    )
    out_specs = (P("tensor", "pipe"), P("pipe", "tensor"), P("pipe", "tensor"), P("tensor", "pipe"))
    return jax.shard_map(
        functools.partial(shards, Axes(mesh)), mesh=mesh, in_specs=in_specs, out_specs=out_specs, check_vma=False
    )
```

```python
import functools

import jax
import jax.numpy as jnp
from jax import lax
from jax.experimental import pallas as pl
from jax.experimental.pallas import tpu as pltpu
from jax.sharding import PartitionSpec as P

BLOCK = 128
BF16 = jnp.bfloat16
F32 = jnp.float32
VMEM_BYTES = 60 * 1024 * 1024
NT = (((1,), (1,)), ((), ()))
NN = (((1,), (0,)), ((), ()))


def params():
    return pltpu.CompilerParams(vmem_limit_bytes=VMEM_BYTES)


def after(x, *others):
    return lax.optimization_barrier((x, *others))[0]


def nothing(x):
    return x[(0,) * x.ndim].astype(F32) * 0.0


def step_of(hid):
    return 512 if hid % 512 == 0 else 256


def chunk_of(size, most):
    return max(c for c in (128, 256, 512, 1024) if size % c == 0 and c <= most)


def ring_of(chips):
    return [0] + list(range(1, chips, 2)) + [c for c in range(chips - 1, 0, -1) if c % 2 == 0]


class Axes:
    def __init__(self, mesh):
        self.pipe = mesh.shape["pipe"]
        self.tensor = mesh.shape["tensor"]
        self.chips = self.tensor // 2
        self.ring = ring_of(self.chips)

    def slots(self):
        n = self.chips
        table = [[self.ring[(self.ring.index(c) - s) % n] for s in range(n)] for c in range(n)]
        return lax.dynamic_slice(jnp.array(table, jnp.int32), (lax.axis_index("tensor") // 2, 0), (1, n))[0]

    def rows(self, tok):
        chip = self.slots() * 2
        core = (lax.axis_index("tensor") % 2).astype(jnp.int32)
        mine, other = (chip + core) * tok, (chip + 1 - core) * tok
        place = lax.axis_index("pipe").astype(jnp.int32).reshape(1)
        return jnp.concatenate([mine[:1], other[:1], mine[1:], other[1:], place])

    def to_core(self, x):
        return lax.ppermute(x, "tensor", [(t, t ^ 1) for t in range(self.tensor)])

    def to_pipe(self, x, bit):
        return lax.ppermute(x, "pipe", [(i, i ^ bit) for i in range(self.pipe)])

    def to_next(self, x):
        pairs = [(self.ring[i], self.ring[(i + 1) % self.chips]) for i in range(self.chips)]
        return lax.ppermute(x, "tensor", [(2 * a + k, 2 * b + k) for a, b in pairs for k in range(2)])


def reduce_over_pipe(axes, partial):
    place = lax.axis_index("pipe")
    bits = axes.pipe.bit_length() - 1
    rows, cols = partial.shape
    left = partial.reshape((2,) * bits + (rows // axes.pipe, cols))
    for i in range(bits):
        axis = bits - 1 - i
        here = (place >> i) % 2
        send = lax.dynamic_slice_in_dim(left, 1 - here, 1, axis).astype(BF16)
        keep = lax.dynamic_slice_in_dim(left, here, 1, axis)
        left = keep + axes.to_pipe(send, 1 << i).astype(F32)
    held = {0: left.reshape(rows // axes.pipe, cols).astype(BF16)}
    for i in reversed(range(bits)):
        for r in list(held):
            held[r ^ (1 << i)] = axes.to_pipe(held[r], 1 << i)
    return [(held[r], r, 0) for r in range(axes.pipe)]


class Square:
    def __init__(self, axes, partial):
        self.axes, self.partial = axes, partial
        self.part = partial.shape[0] // 4
        self.half = self.part // 2

    def block(self, r, first, count):
        at = ((lax.axis_index("pipe") ^ r) * self.part + first, 0)
        return lax.dynamic_slice(self.partial, at, (count, self.partial.shape[1]))

    def send(self, for_1, for_2, others):
        for_1, for_2 = lax.optimization_barrier((for_1, for_2, *others))[:2] if others else (for_1, for_2)
        return self.axes.to_pipe(for_1, 1), self.axes.to_pipe(for_2, 2)

    def corner(self, others):
        half = self.half
        self.by = self.send(self.block(3, 0, half).astype(BF16), self.block(3, half, half).astype(BF16), others)

    def sides(self, others):
        half = self.half
        by_1, by_2 = [a.astype(F32) for a in self.by]
        for_1 = jnp.concatenate([self.block(1, 0, half), self.block(1, half, half) + by_2], axis=0).astype(BF16)
        for_2 = jnp.concatenate([self.block(2, 0, half) + by_1, self.block(2, half, half)], axis=0).astype(BF16)
        self.terms = self.send(for_1, for_2, others)

    def back(self, others, zero=0.0):
        mine = self.block(0, 0, self.part) + self.terms[0].astype(F32) + self.terms[1].astype(F32)
        self.mine = (mine + zero).astype(BF16)
        self.near = self.send(self.mine, self.mine, others)

    def across(self, others, zero=0.0):
        for_1, for_2 = self.near[1][self.half :], self.near[0][: self.half]
        self.far = self.send(for_1 + jnp.asarray(zero, BF16), for_2 + jnp.asarray(zero, BF16), others)

    def back_at_once(self):
        mine = self.block(0, 0, self.part) + self.terms[0].astype(F32) + self.terms[1].astype(F32)
        self.mine = mine.astype(BF16)
        self.near = self.send(self.mine, self.mine, [])
        self.far = self.axes.to_pipe(self.mine, 3)

    def result(self):
        if not isinstance(self.far, tuple):
            return [(self.mine, 0, 0), (self.near[0], 1, 0), (self.near[1], 2, 0), (self.far, 3, 0)]
        return [
            (self.mine, 0, 0),
            (self.near[0], 1, 0),
            (self.near[1], 2, 0),
            (self.far[1], 3, 0),
            (self.far[0], 3, self.half),
        ]


def sigmoid(g):
    return 0.5 + 0.5 * jnp.tanh(0.5 * g)


def grads_kernel(cfg, at_rows, *refs):
    refs = list(refs)
    take = lambda n: [refs.pop(0) for _ in range(n)]
    parts = take(len(cfg["sources"]))
    gate_pre, up_pre, gate_w, up_w, gate_m, up_m = take(6)
    acc_in = take(1)[0] if cfg["acc_in"] else None
    gate_out, up_out, acc, hidden, both = refs
    step, tok, chunk = cfg["step"], cfg["tok"], cfg["chunk"]
    k = pl.program_id(0)
    place = at_rows[cfg["groups"]]

    for (r, first), ref in zip(cfg["sources"], parts):
        to = (place ^ r) * cfg["part"] + first
        hidden[pl.ds(pl.multiple_of(to, 16), ref.shape[0]), :] = ref[...]
    for i in range(cfg["groups"]):
        at = pl.ds(pl.multiple_of(at_rows[i], 16), tok)
        g = gate_pre[at, :].astype(F32)
        u = up_pre[at, :].astype(F32)
        h = hidden[i * tok : (i + 1) * tok, :].astype(F32)
        sig = sigmoid(g)
        h = h * sig
        gg = (h * u * (1.0 + g * (1.0 - sig))).astype(BF16)
        ug = (h * g).astype(BF16)
        gate_out[at, :] = gg
        up_out[at, :] = ug
        both[at, :step] = gg
        both[at, step:] = ug

    def tile(n, first):
        def masked(w, m):
            rows = []
            for i in range(chunk // BLOCK):
                at = pl.ds(pl.multiple_of(n * chunk + i * BLOCK, BLOCK), BLOCK)
                rows.append(w[at, :] * m[pl.ds(n * (chunk // BLOCK) + i, 1), :].astype(BF16))
            return jnp.concatenate(rows, axis=0)

        w = jnp.concatenate([masked(gate_w, gate_m), masked(up_w, up_m)], axis=1)
        to = pl.ds(pl.multiple_of(n * chunk, chunk), chunk)
        term = lax.dot_general(both[...], w, NT, preferred_element_type=F32)
        if not first:
            term += acc[:, to]
        elif acc_in is not None:
            term += acc_in[:, to]
        acc[:, to] = term

    tiles = cfg["width"] // chunk

    @pl.when(k == 0)
    def _():
        pl.loop(0, tiles)(lambda n: tile(n, True))

    @pl.when(k > 0)
    def _():
        pl.loop(0, tiles)(lambda n: tile(n, False))


def local_grads(axes, at_rows, sources, gate_pre, up_pre, gate_w, up_w, gate_m, up_m, acc, tok, start, cols):
    tokens, hid = gate_pre.shape
    width = gate_w.shape[0]
    step = step_of(hid)
    first = start // step
    col = lambda k, _: (0, first + k)
    one = lambda k, _: (0, 0)
    own = lambda k, _: (0, k)
    specs = [pl.BlockSpec((a.shape[0], step), own) for a, _, _ in sources]
    specs += [pl.BlockSpec((tokens, step), col)] * 2
    specs += [pl.BlockSpec((width, step), col)] * 2
    specs += [pl.BlockSpec((gate_m.shape[0], step), col)] * 2
    arrays = [a for a, _, _ in sources] + [gate_pre, up_pre, gate_w, up_w, gate_m, up_m]
    if acc is not None:
        specs.append(pl.BlockSpec((tokens, width), one, pipeline_mode=pl.Buffered(1)))
        arrays.append(acc)
    cfg = dict(
        sources=[(r, lo) for _, r, lo in sources], part=tokens // axes.pipe, groups=tokens // tok, tok=tok, step=step,
        width=width, chunk=chunk_of(width, 1024), acc_in=acc is not None,
    )
    return pl.pallas_call(
        functools.partial(grads_kernel, cfg),
        out_shape=[jax.ShapeDtypeStruct((tokens, cols), BF16)] * 2 + [jax.ShapeDtypeStruct((tokens, width), F32)],
        grid_spec=pltpu.PrefetchScalarGridSpec(
            num_scalar_prefetch=1,
            grid=(cols // step,),
            in_specs=specs,
            out_specs=[pl.BlockSpec((tokens, step), own)] * 2 + [pl.BlockSpec((tokens, width), one)],
            scratch_shapes=[pltpu.VMEM((tokens, step), BF16), pltpu.VMEM((tokens, 2 * step), BF16)],
        ),
        compiler_params=params(),
        cost_estimate=pl.CostEstimate(
            flops=4 * tokens * width * cols,
            bytes_accessed=4 * width * cols + 10 * tokens * cols + 8 * tokens * width,
            transcendentals=tokens * cols,
        ),
        name="local_grads",
    )(at_rows, *arrays)


def weights_kernel(cfg, x, gate, up, gate_m, up_m, *refs):
    *outs, done = refs[-3:]
    done[...] = jnp.zeros_like(done)
    chunk = cfg["chunk"]
    for g, m, out in ((gate, gate_m, outs[0]), (up, up_m, outs[1])):

        def tile(n, g=g, m=m, out=out):
            at = pl.ds(pl.multiple_of(n * chunk, chunk), chunk)
            term = lax.dot_general(x[at, :], g[...], NN, preferred_element_type=F32)
            for i in range(chunk // BLOCK):
                to = pl.ds(pl.multiple_of(n * chunk + i * BLOCK, BLOCK), BLOCK)
                row = m[pl.ds(n * (chunk // BLOCK) + i, 1), :]
                out[to, :] = (term[i * BLOCK : (i + 1) * BLOCK, :] * row).astype(BF16)

        pl.loop(0, cfg["width"] // chunk)(tile)


def weight_grads(x_t, gate, up, gate_m, up_m, before, shape, start, skip, steps):
    width, tokens = x_t.shape
    step = step_of(shape[1])
    first = start // step + skip
    col = lambda k: (0, first + k)
    specs = [
        pl.BlockSpec((width, tokens), lambda k: (0, 0), pipeline_mode=pl.Buffered(1)),
        pl.BlockSpec((tokens, step), lambda k: (0, skip + k)),
        pl.BlockSpec((tokens, step), lambda k: (0, skip + k)),
        pl.BlockSpec((gate_m.shape[0], step), col),
        pl.BlockSpec((gate_m.shape[0], step), col),
    ]
    arrays = [x_t, gate, up, gate_m, up_m]
    alias = {}
    if before is not None:
        specs += [pl.BlockSpec(memory_space=pl.ANY)] * 2
        arrays += list(before)
        alias = {5: 0, 6: 1}
    return pl.pallas_call(
        functools.partial(weights_kernel, dict(width=width, chunk=chunk_of(width, 1024))),
        out_shape=[jax.ShapeDtypeStruct(shape, BF16)] * 2 + [jax.ShapeDtypeStruct((8, 128), F32)],
        grid=(steps,),
        in_specs=specs,
        out_specs=[pl.BlockSpec((width, step), col)] * 2 + [pl.BlockSpec((8, 128), lambda k: (0, 0))],
        input_output_aliases=alias,
        compiler_params=params(),
        cost_estimate=pl.CostEstimate(
            flops=4 * tokens * width * steps * step,
            bytes_accessed=4 * (width + tokens) * steps * step + 2 * tokens * width,
            transcendentals=0,
        ),
        name="weight_grads",
    )(*arrays)


def down_kernel(cfg, at_rows, *refs):
    rows, gate_pre, up_pre, mask = refs[:4]
    out, done, hidden = refs[-3:]
    tok = cfg["tok"]
    done[...] = jnp.zeros_like(done)
    for i in range(cfg["groups"]):
        at = pl.ds(pl.multiple_of(at_rows[i], 16), tok)
        g = gate_pre[at, :].astype(F32)
        u = up_pre[at, :].astype(F32)
        hidden[i * tok : (i + 1) * tok, :] = (g * sigmoid(g) * u).astype(BF16)
    across = hidden[...].T
    chunk = cfg["chunk"]

    def tile(n):
        at = pl.ds(pl.multiple_of(n * chunk, chunk), chunk)
        term = lax.dot_general(across, rows[:, at], NN, preferred_element_type=F32)
        for i in range(cfg["step"] // BLOCK):
            part = slice(i * BLOCK, (i + 1) * BLOCK)
            out[part, at] = (term[part, :] * mask[i, :, at]).astype(BF16)

    pl.loop(0, cfg["width"] // chunk)(tile)


def down_grad(at_rows, rows, gate_pre, up_pre, mask, tok, before, first, last):
    tokens, hid = gate_pre.shape
    width = rows.shape[1]
    step = step_of(hid)
    cfg = dict(groups=tokens // tok, tok=tok, width=width, step=step, chunk=chunk_of(width, 1024))
    specs = [pl.BlockSpec(rows.shape, lambda k, _: (0, 0), pipeline_mode=pl.Buffered(1))]
    specs += [pl.BlockSpec((tokens, step), lambda k, _: (0, first + k))] * 2
    specs += [pl.BlockSpec((step // BLOCK, 1, width), lambda k, _: (first + k, 0, 0))]
    arrays = [rows, gate_pre, up_pre, mask]
    alias = {}
    if before is not None:
        specs.append(pl.BlockSpec(memory_space=pl.ANY))
        arrays.append(before)
        alias = {len(arrays): 0}
    cols = (last - first) * step
    return pl.pallas_call(
        functools.partial(down_kernel, cfg),
        out_shape=[jax.ShapeDtypeStruct((hid, width), BF16), jax.ShapeDtypeStruct((8, 128), F32)],
        grid_spec=pltpu.PrefetchScalarGridSpec(
            num_scalar_prefetch=1,
            grid=(last - first,),
            in_specs=specs,
            out_specs=[
                pl.BlockSpec((step, width), lambda k, _: (first + k, 0)),
                pl.BlockSpec((8, 128), lambda k, _: (0, 0)),
            ],
            scratch_shapes=[pltpu.VMEM((tokens, step), BF16)],
        ),
        input_output_aliases=alias,
        compiler_params=params(),
        cost_estimate=pl.CostEstimate(
            flops=2 * tokens * width * cols,
            bytes_accessed=2 * (tokens * width + 2 * tokens * cols + width * cols),
            transcendentals=tokens * cols,
        ),
        name="down_grad",
    )(at_rows, *arrays)


def masked(weight, mask):
    rows, cols = weight.shape
    return (weight.reshape(rows // BLOCK, BLOCK, cols) * mask.astype(BF16)[:, None, :]).reshape(rows, cols)


def dot_nt(a, b):
    return lax.dot_general(a, b, NT, preferred_element_type=F32)


def shards(axes, layer_input, out_grad, gate_pre, up_pre, gate_weight, up_weight, down_weight, gate_mask, up_mask, down_mask):
    tokens, hid = gate_pre.shape
    tok, width = out_grad.shape
    step = step_of(hid)
    steps = hid // step
    first = (steps + 1) // 2 * step
    pieces = [(0, first), (first, hid - first)]
    at_rows = axes.rows(tok)
    gate_m = jnp.repeat(gate_mask, BLOCK, axis=1).astype(F32)
    up_m = jnp.repeat(up_mask, BLOCK, axis=1).astype(F32)
    down_m = jnp.repeat(down_mask, BLOCK, axis=1).astype(F32)

    near = [out_grad, axes.to_core(out_grad)]
    downs = [masked(down_weight[c : c + w], down_m[c // BLOCK : (c + w) // BLOCK]) for c, w in pieces]
    half = tok // 2
    now, got = [out_grad[:half], out_grad[half:]], []
    for s in range(axes.chips - 1):
        if s == 2:
            now = lax.optimization_barrier((*now, downs[0]))[:2]
        now = [axes.to_next(a) for a in now]
        got += now
    rows = jnp.concatenate(near + got + [axes.to_core(a) for a in got], axis=0)

    x = lax.all_gather(after(layer_input, rows), "tensor", axis=0, tiled=True)
    down = functools.partial(down_grad, rows=rows, gate_pre=gate_pre, up_pre=up_pre, mask=down_m[:, None, :], tok=tok)
    if axes.pipe == 4:
        squares = []
        for i, d in enumerate(downs):
            prev = squares[i - 1] if i else None
            sq = Square(axes, dot_nt(after(rows, *prev.by) if i else rows, d))
            squares.append(sq)
            sq.corner(prev.by if i else [])
            if not i:
                grad_down, done = down(after(at_rows, *sq.by), before=None, first=0, last=(steps + 1) // 2)
            sq.sides(prev.terms if i else [])
            if i:
                sq.back_at_once()
                continue
            sq.back([], done[0, 0])
            grad_down, done = down(after(at_rows, *sq.terms), before=grad_down, first=(steps + 1) // 2, last=steps)
            sq.across([], done[0, 0])
        at_rows = at_rows + nothing(squares[-1].mine).astype(jnp.int32)
        sums = [sq.result() for sq in squares]
    else:
        parts = [dot_nt(rows, d) for d in downs]
        sums = [reduce_over_pipe(axes, p) for p in parts]
        grad_down, _ = down(after(at_rows, *parts), before=None, first=0, last=steps)
    x_t = x.T
    at_rows = at_rows + nothing(x_t).astype(jnp.int32)

    acc, grads = None, []
    for (c, w), sources in zip(pieces, sums):
        gate, up, acc = local_grads(
            axes, at_rows, sources, gate_pre, up_pre, gate_weight, up_weight, gate_m, up_m, acc, tok, c, w
        )
        grads.append((gate, up))

    core = lax.axis_index("tensor") % 2
    slots = axes.slots()
    by_core = acc.reshape(axes.chips, 2, tok, width)
    pick = lambda a, i, axis: lax.dynamic_index_in_dim(a, i, axis, keepdims=False)
    total = pick(by_core, core, 1) + axes.to_core(pick(by_core, 1 - core, 1))

    todo = [(c, g, skip, min(2, w // step - skip)) for (c, w), g in zip(pieces, grads) for skip in range(0, w // step, 2)]
    weights = None

    def weights_part(zero):
        nonlocal weights
        c, (gate, up), skip, count = todo.pop(0)
        weights = weight_grads(x_t, gate, up, gate_m, up_m + zero, weights, gate_weight.shape, c, skip, count)
        *weights, done = weights
        return done[0, 0]

    weights_part(0.0)
    run = pick(total, slots[1 % axes.chips], 0).astype(BF16)
    for s in range(1, axes.chips):
        zero = weights_part(nothing(run)) if todo else 0.0
        run = axes.to_next(run).astype(F32) + pick(total, slots[(s + 1) % axes.chips], 0) + zero
        run = run.astype(BF16)
    while todo:
        weights_part(0.0)
    return (run, weights[0], weights[1], grad_down)


def solution(mesh):
    in_specs = (
        P("tensor", "pipe"),
        P("tensor", "pipe"),
        P(None, "tensor"),
        P(None, "tensor"),
        P("pipe", "tensor"),
        P("pipe", "tensor"),
        P("tensor", "pipe"),
        P("pipe", "tensor"),
        P("pipe", "tensor"),
        P("tensor", "pipe"),
    )
    out_specs = (P("tensor", "pipe"), P("pipe", "tensor"), P("pipe", "tensor"), P("tensor", "pipe"))
    return jax.shard_map(
        functools.partial(shards, Axes(mesh)), mesh=mesh, in_specs=in_specs, out_specs=out_specs, check_vma=False
    )
```

```python
import functools

import jax
import jax.numpy as jnp
from jax import lax
from jax.experimental import pallas as pl
from jax.experimental.pallas import tpu as pltpu
from jax.sharding import PartitionSpec as P

BLOCK = 128
BF16 = jnp.bfloat16
F32 = jnp.float32
VMEM_BYTES = 60 * 1024 * 1024
NT = (((1,), (1,)), ((), ()))
NN = (((1,), (0,)), ((), ()))


def params():
    return pltpu.CompilerParams(vmem_limit_bytes=VMEM_BYTES)


def after(x, *others):
    return lax.optimization_barrier((x, *others))[0]


def nothing(x):
    return x[(0,) * x.ndim].astype(F32) * 0.0


def step_of(hid):
    return 512 if hid % 512 == 0 else 256


def chunk_of(size, most):
    return max(c for c in (128, 256, 512, 1024) if size % c == 0 and c <= most)


def ring_of(chips):
    return [0] + list(range(1, chips, 2)) + [c for c in range(chips - 1, 0, -1) if c % 2 == 0]


class Axes:
    def __init__(self, mesh):
        self.pipe = mesh.shape["pipe"]
        self.tensor = mesh.shape["tensor"]
        self.chips = self.tensor // 2
        self.ring = ring_of(self.chips)

    def slots(self):
        n = self.chips
        table = [[self.ring[(self.ring.index(c) - s) % n] for s in range(n)] for c in range(n)]
        return lax.dynamic_slice(jnp.array(table, jnp.int32), (lax.axis_index("tensor") // 2, 0), (1, n))[0]

    def rows(self, tok):
        chip = self.slots() * 2
        core = (lax.axis_index("tensor") % 2).astype(jnp.int32)
        mine, other = (chip + core) * tok, (chip + 1 - core) * tok
        place = lax.axis_index("pipe").astype(jnp.int32).reshape(1)
        return jnp.concatenate([mine[:1], other[:1], mine[1:], other[1:], place])

    def to_core(self, x):
        return lax.ppermute(x, "tensor", [(t, t ^ 1) for t in range(self.tensor)])

    def to_pipe(self, x, bit):
        return lax.ppermute(x, "pipe", [(i, i ^ bit) for i in range(self.pipe)])

    def to_next(self, x):
        pairs = [(self.ring[i], self.ring[(i + 1) % self.chips]) for i in range(self.chips)]
        return lax.ppermute(x, "tensor", [(2 * a + k, 2 * b + k) for a, b in pairs for k in range(2)])


def reduce_over_pipe(axes, partial):
    place = lax.axis_index("pipe")
    bits = axes.pipe.bit_length() - 1
    rows, cols = partial.shape
    left = partial.reshape((2,) * bits + (rows // axes.pipe, cols))
    for i in range(bits):
        axis = bits - 1 - i
        here = (place >> i) % 2
        send = lax.dynamic_slice_in_dim(left, 1 - here, 1, axis).astype(BF16)
        keep = lax.dynamic_slice_in_dim(left, here, 1, axis)
        left = keep + axes.to_pipe(send, 1 << i).astype(F32)
    held = {0: left.reshape(rows // axes.pipe, cols).astype(BF16)}
    for i in reversed(range(bits)):
        for r in list(held):
            held[r ^ (1 << i)] = axes.to_pipe(held[r], 1 << i)
    return [(held[r], r, 0) for r in range(axes.pipe)]


class Square:
    def __init__(self, axes, partial):
        self.axes, self.partial = axes, partial
        self.part = partial.shape[0] // 4
        self.half = self.part // 2

    def block(self, r, first, count):
        at = ((lax.axis_index("pipe") ^ r) * self.part + first, 0)
        return lax.dynamic_slice(self.partial, at, (count, self.partial.shape[1]))

    def send(self, for_1, for_2, others):
        for_1, for_2 = lax.optimization_barrier((for_1, for_2, *others))[:2] if others else (for_1, for_2)
        return self.axes.to_pipe(for_1, 1), self.axes.to_pipe(for_2, 2)

    def corner(self, others):
        half = self.half
        self.by = self.send(self.block(3, 0, half).astype(BF16), self.block(3, half, half).astype(BF16), others)

    def sides(self, others):
        half = self.half
        by_1, by_2 = [a.astype(F32) for a in self.by]
        for_1 = jnp.concatenate([self.block(1, 0, half), self.block(1, half, half) + by_2], axis=0).astype(BF16)
        for_2 = jnp.concatenate([self.block(2, 0, half) + by_1, self.block(2, half, half)], axis=0).astype(BF16)
        self.terms = self.send(for_1, for_2, others)

    def back(self, zero=0.0):
        mine = self.block(0, 0, self.part) + self.terms[0].astype(F32) + self.terms[1].astype(F32)
        self.mine = (mine + zero).astype(BF16)
        self.others = [(self.axes.to_pipe(self.mine, r), r, 0) for r in (1, 2, 3)]

    def result(self):
        return [(self.mine, 0, 0), *self.others]


def sigmoid(g):
    return 0.5 + 0.5 * jnp.tanh(0.5 * g)


def grads_kernel(cfg, at_rows, *refs):
    count = len(cfg["sources"])
    parts = refs[:count]
    gate_pre, up_pre, gate_w, up_w, gate_m, up_m = refs[count : count + 6]
    acc_in = refs[count + 6 : count + 10] if cfg["acc_in"] else None
    out, *acc, hidden, both = refs[-7:]
    step, tok, chunk = cfg["step"], cfg["tok"], cfg["chunk"]
    place = at_rows[cfg["groups"]]

    for (r, first), ref in zip(cfg["sources"], parts):
        to = (place ^ r) * cfg["part"] + first
        hidden[pl.ds(pl.multiple_of(to, 16), ref.shape[0]), :] = ref[...]
    for i in range(cfg["groups"]):
        at = pl.ds(pl.multiple_of(at_rows[i], 16), tok)
        rows = slice(i * tok, (i + 1) * tok)
        g = gate_pre[at, :].astype(F32)
        u = up_pre[at, :].astype(F32)
        h = hidden[rows, :].astype(F32)
        sig = sigmoid(g)
        h = h * sig
        gg = (h * u * (1.0 + g * (1.0 - sig))).astype(BF16)
        ug = (h * g).astype(BF16)
        out[at, :step] = gg
        out[at, step:] = ug
        both[rows, :step] = gg
        both[rows, step:] = ug

    @pl.when(pl.program_id(0) == 0)
    def _():
        for i, ref in enumerate(acc):
            ref[...] = jnp.zeros_like(ref) if acc_in is None else acc_in[i][...]

    def masked(w, m, at):
        rows = [
            w[at + i : at + i + BLOCK, :] * m[(at + i) // BLOCK : (at + i) // BLOCK + 1, :].astype(BF16)
            for i in range(0, chunk, BLOCK)
        ]
        return jnp.concatenate(rows, axis=0)

    for at in range(0, cfg["width"], chunk):
        w = jnp.concatenate([masked(gate_w, gate_m, at), masked(up_w, up_m, at)], axis=1)
        term = lax.dot_general(both[...], w, NT, preferred_element_type=F32)
        lo = 0
        for ref in acc:
            ref[:, at : at + chunk] += term[lo : lo + ref.shape[0], :]
            lo += ref.shape[0]


def local_grads(axes, at_rows, sources, gate_pre, up_pre, gate_w, up_w, gate_m, up_m, acc, tok, start, cols, ties):
    tokens, hid = gate_pre.shape
    width = gate_w.shape[0]
    step = step_of(hid)
    first = start // step
    col = lambda k, _: (0, first + k)
    one = lambda k, _: (0, 0)
    own = lambda k, _: (0, k)
    groups = [tok, tok, tokens // 2 - tok, tokens // 2 - tok]
    specs = [pl.BlockSpec((a.shape[0], step), own) for a, _, _ in sources]
    specs += [pl.BlockSpec((tokens, step), col)] * 2
    specs += [pl.BlockSpec((width, step), col)] * 2
    specs += [pl.BlockSpec((gate_m.shape[0], step), col)] * 2
    arrays = [a for a, _, _ in sources] + [gate_pre, up_pre, gate_w, up_w, gate_m, up_m]
    if acc is not None:
        specs += [pl.BlockSpec((n, width), one, pipeline_mode=pl.Buffered(1)) for n in groups]
        arrays += acc
    specs += [pl.BlockSpec(memory_space=pl.ANY)] * len(ties)
    arrays += ties
    cfg = dict(
        sources=[(r, lo) for _, r, lo in sources], part=tokens // axes.pipe, groups=tokens // tok, tok=tok, step=step,
        width=width, chunk=chunk_of(width, 1024), acc_in=acc is not None,
    )
    out = pl.pallas_call(
        functools.partial(grads_kernel, cfg),
        out_shape=[jax.ShapeDtypeStruct((tokens, 2 * cols), BF16)]
        + [jax.ShapeDtypeStruct((n, width), F32) for n in groups],
        grid_spec=pltpu.PrefetchScalarGridSpec(
            num_scalar_prefetch=1,
            grid=(cols // step,),
            in_specs=specs,
            out_specs=[pl.BlockSpec((tokens, 2 * step), own)] + [pl.BlockSpec((n, width), one) for n in groups],
            scratch_shapes=[pltpu.VMEM((tokens, step), BF16), pltpu.VMEM((tokens, 2 * step), BF16)],
        ),
        compiler_params=params(),
        cost_estimate=pl.CostEstimate(
            flops=4 * tokens * width * cols,
            bytes_accessed=4 * width * cols + 10 * tokens * cols + 8 * tokens * width,
            transcendentals=tokens * cols,
        ),
        name="local_grads",
    )(at_rows, *arrays)
    return out[0], list(out[1:])


def weights_kernel(cfg, x, grads, gate_m, up_m, *refs):
    gate_out, up_out, done = refs[-3:]
    done[...] = jnp.zeros_like(done)
    chunk, step = cfg["chunk"], cfg["step"]
    for at in range(0, cfg["width"], chunk):
        term = lax.dot_general(x[at : at + chunk, :], grads[...], NN, preferred_element_type=F32)
        for i in range(0, chunk, BLOCK):
            rows = slice(at + i, at + i + BLOCK)
            block = (at + i) // BLOCK
            gate_out[rows, :] = (term[i : i + BLOCK, :step] * gate_m[block : block + 1, :]).astype(BF16)
            up_out[rows, :] = (term[i : i + BLOCK, step:] * up_m[block : block + 1, :]).astype(BF16)


def weight_grads(x_t, grads, gate_m, up_m, before, shape, start, skip, steps, ties):
    width, tokens = x_t.shape
    step = step_of(shape[1])
    first = start // step + skip
    col = lambda k: (0, first + k)
    specs = [
        pl.BlockSpec((width, tokens), lambda k: (0, 0), pipeline_mode=pl.Buffered(1)),
        pl.BlockSpec((tokens, 2 * step), lambda k: (0, skip + k)),
        pl.BlockSpec((gate_m.shape[0], step), col),
        pl.BlockSpec((gate_m.shape[0], step), col),
    ]
    arrays = [x_t, grads, gate_m, up_m]
    alias = {}
    if before is not None:
        specs += [pl.BlockSpec(memory_space=pl.ANY)] * 2
        arrays += list(before)
        alias = {4: 0, 5: 1}
    specs += [pl.BlockSpec(memory_space=pl.ANY)] * len(ties)
    arrays += ties
    *out, done = pl.pallas_call(
        functools.partial(weights_kernel, dict(width=width, chunk=chunk_of(width, 512), step=step)),
        out_shape=[jax.ShapeDtypeStruct(shape, BF16)] * 2 + [jax.ShapeDtypeStruct((8, 128), F32)],
        grid=(steps,),
        in_specs=specs,
        out_specs=[pl.BlockSpec((width, step), col)] * 2 + [pl.BlockSpec((8, 128), lambda k: (0, 0))],
        input_output_aliases=alias,
        compiler_params=params(),
        cost_estimate=pl.CostEstimate(
            flops=4 * tokens * width * steps * step,
            bytes_accessed=4 * (width + tokens) * steps * step + 2 * tokens * width,
            transcendentals=0,
        ),
        name="weight_grads",
    )(*arrays)
    return out, done


def down_kernel(cfg, at_rows, *refs):
    rows, gate_pre, up_pre, mask = refs[:4]
    out, done, hidden = refs[-3:]
    tok = cfg["tok"]
    done[...] = jnp.zeros_like(done)
    for i in range(cfg["groups"]):
        at = pl.ds(pl.multiple_of(at_rows[i], 16), tok)
        g = gate_pre[at, :].astype(F32)
        u = up_pre[at, :].astype(F32)
        hidden[i * tok : (i + 1) * tok, :] = (g * sigmoid(g) * u).astype(BF16)
    across = hidden[...].T
    chunk = cfg["chunk"]

    for lo in range(0, cfg["width"], chunk):
        at = slice(lo, lo + chunk)
        term = lax.dot_general(across, rows[:, at], NN, preferred_element_type=F32)
        for i in range(cfg["step"] // BLOCK):
            part = slice(i * BLOCK, (i + 1) * BLOCK)
            out[part, at] = (term[part, :] * mask[i, :, at]).astype(BF16)


def down_grad(at_rows, rows, gate_pre, up_pre, mask, tok, before, first, last, ties):
    tokens, hid = gate_pre.shape
    width = rows.shape[1]
    step = step_of(hid)
    cfg = dict(groups=tokens // tok, tok=tok, width=width, step=step, chunk=chunk_of(width, 1024))
    specs = [pl.BlockSpec(rows.shape, lambda k, _: (0, 0), pipeline_mode=pl.Buffered(1))]
    specs += [pl.BlockSpec((tokens, step), lambda k, _: (0, first + k))] * 2
    specs += [pl.BlockSpec((step // BLOCK, 1, width), lambda k, _: (first + k, 0, 0))]
    arrays = [rows, gate_pre, up_pre, mask]
    alias = {}
    if before is not None:
        specs.append(pl.BlockSpec(memory_space=pl.ANY))
        arrays.append(before)
        alias = {len(arrays): 0}
    specs += [pl.BlockSpec(memory_space=pl.ANY)] * len(ties)
    arrays += ties
    cols = (last - first) * step
    return pl.pallas_call(
        functools.partial(down_kernel, cfg),
        out_shape=[jax.ShapeDtypeStruct((hid, width), BF16), jax.ShapeDtypeStruct((8, 128), F32)],
        grid_spec=pltpu.PrefetchScalarGridSpec(
            num_scalar_prefetch=1,
            grid=(last - first,),
            in_specs=specs,
            out_specs=[
                pl.BlockSpec((step, width), lambda k, _: (first + k, 0)),
                pl.BlockSpec((8, 128), lambda k, _: (0, 0)),
            ],
            scratch_shapes=[pltpu.VMEM((tokens, step), BF16)],
        ),
        input_output_aliases=alias,
        compiler_params=params(),
        cost_estimate=pl.CostEstimate(
            flops=2 * tokens * width * cols,
            bytes_accessed=2 * (tokens * width + 2 * tokens * cols + width * cols),
            transcendentals=tokens * cols,
        ),
        name="down_grad",
    )(at_rows, *arrays)


def masked(weight, mask):
    rows, cols = weight.shape
    return (weight.reshape(rows // BLOCK, BLOCK, cols) * mask.astype(BF16)[:, None, :]).reshape(rows, cols)


def dot_nt(a, b):
    return lax.dot_general(a, b, NT, preferred_element_type=F32)


def shards(axes, layer_input, out_grad, gate_pre, up_pre, gate_weight, up_weight, down_weight, gate_mask, up_mask, down_mask):
    tokens, hid = gate_pre.shape
    tok, width = out_grad.shape
    step = step_of(hid)
    steps = hid // step
    counts = [2, steps - 4, 2] if steps > 4 else [steps]
    pieces = [(sum(counts[:i]) * step, n * step) for i, n in enumerate(counts)]
    at_rows = axes.rows(tok)
    gate_m = jnp.repeat(gate_mask, BLOCK, axis=1).astype(F32)
    up_m = jnp.repeat(up_mask, BLOCK, axis=1).astype(F32)
    down_m = jnp.repeat(down_mask, BLOCK, axis=1).astype(F32)

    near = [out_grad, axes.to_core(out_grad)]
    downs = [masked(down_weight[c : c + w], down_m[c // BLOCK : (c + w) // BLOCK]) for c, w in pieces]
    half = tok // 2
    now, got = [out_grad[:half], out_grad[half:]], []
    for s in range(axes.chips - 1):
        if s == 1:
            now[1] = after(now[1], *downs)
        now = [axes.to_next(a) for a in now]
        got += now
    rows = jnp.concatenate(near + got + [axes.to_core(a) for a in got], axis=0)

    x = lax.all_gather(after(layer_input, rows), "tensor", axis=0, tiled=True)
    down = functools.partial(down_grad, rows=rows, gate_pre=gate_pre, up_pre=up_pre, mask=down_m[:, None, :], tok=tok)
    half_steps = (steps + 1) // 2
    if axes.pipe == 4:
        squares = []
        for i, d in enumerate(downs):
            prev = squares[i - 1] if i else None
            sq = Square(axes, dot_nt(after(rows, *prev.by) if i else rows, d))
            squares.append(sq)
            sq.corner(prev.by if i else [])
            sq.sides(prev.terms if i else [])
            if not i:
                grad_down, done = down(at_rows, before=None, first=0, last=half_steps, ties=list(sq.by))
            sq.back(0.0 if i else done[0, 0])
        sums = [sq.result() for sq in squares]
    else:
        sums = [reduce_over_pipe(axes, dot_nt(rows, d)) for d in downs]
        grad_down, done = down(at_rows, before=None, first=0, last=half_steps, ties=[])
    x_t = x.T

    acc, grads, weights, waits = None, [], None, []
    for i, ((c, w), sources) in enumerate(zip(pieces, sums)):
        if i + 1 < len(sums):
            waits = waits + [sums[i + 1][0][0]]
        both, acc = local_grads(
            axes, at_rows, sources, gate_pre, up_pre, gate_weight, up_weight, gate_m, up_m, acc, tok, c, w, waits
        )
        grads.append(both)
        waits = []
        if not i:
            weights, ready = weight_grads(
                x_t, both, gate_m, up_m, None, gate_weight.shape, c, 0, w // step, []
            )
            waits = [ready]

    todo = [(i, skip) for i in reversed(range(1, len(pieces))) for skip in range(0, pieces[i][1] // step, 2)]
    todo.insert(1, None)

    def next_part(ties):
        nonlocal weights, grad_down
        part = todo.pop(0)
        if part is None:
            grad_down, _ = down(at_rows, before=grad_down, first=half_steps, last=steps, ties=ties)
            return
        i, skip = part
        c, w = pieces[i]
        weights, _ = weight_grads(
            x_t, grads[i], gate_m, up_m, weights, gate_weight.shape, c, skip, min(2, w // step - skip), ties
        )

    near_own, near_other, far_own, far_other = acc
    far_there, near_there = axes.to_core(far_other), axes.to_core(near_other)
    next_part([])
    run = (far_own[:tok] + far_there[:tok]).astype(BF16)
    for s in range(1, axes.chips):
        if todo:
            next_part([run])
        at = slice(s * tok, (s + 1) * tok)
        term = far_own[at] + far_there[at] if s < axes.chips - 1 else near_own + near_there
        run = (axes.to_next(run).astype(F32) + term).astype(BF16)
    while todo:
        next_part([])
    return (run, weights[0], weights[1], grad_down)


def solution(mesh):
    in_specs = (
        P("tensor", "pipe"),
        P("tensor", "pipe"),
        P(None, "tensor"),
        P(None, "tensor"),
        P("pipe", "tensor"),
        P("pipe", "tensor"),
        P("tensor", "pipe"),
        P("pipe", "tensor"),
        P("pipe", "tensor"),
        P("tensor", "pipe"),
    )
    out_specs = (P("tensor", "pipe"), P("pipe", "tensor"), P("pipe", "tensor"), P("tensor", "pipe"))
    return jax.shard_map(
        functools.partial(shards, Axes(mesh)), mesh=mesh, in_specs=in_specs, out_specs=out_specs, check_vma=False
    )
```

```python
import functools

import jax
import jax.numpy as jnp
from jax import lax
from jax.experimental import pallas as pl
from jax.experimental.pallas import tpu as pltpu
from jax.sharding import PartitionSpec as P

BLOCK = 128
BF16 = jnp.bfloat16
F32 = jnp.float32
VMEM_BYTES = 60 * 1024 * 1024
NT = (((1,), (1,)), ((), ()))
NN = (((1,), (0,)), ((), ()))


def params():
    return pltpu.CompilerParams(vmem_limit_bytes=VMEM_BYTES)


def after(x, *others):
    return lax.optimization_barrier((x, *others))[0]


def nothing(x):
    return x[(0,) * x.ndim].astype(F32) * 0.0


def step_of(hid):
    return 512 if hid % 512 == 0 else 256


def chunk_of(size, most):
    return max(c for c in (128, 256, 512, 1024) if size % c == 0 and c <= most)


def ring_of(chips):
    return [0] + list(range(1, chips, 2)) + [c for c in range(chips - 1, 0, -1) if c % 2 == 0]


class Axes:
    def __init__(self, mesh):
        self.pipe = mesh.shape["pipe"]
        self.tensor = mesh.shape["tensor"]
        self.chips = self.tensor // 2
        self.ring = ring_of(self.chips)

    def slots(self):
        n = self.chips
        table = [[self.ring[(self.ring.index(c) - s) % n] for s in range(n)] for c in range(n)]
        return lax.dynamic_slice(jnp.array(table, jnp.int32), (lax.axis_index("tensor") // 2, 0), (1, n))[0]

    def rows(self, tok):
        chip = self.slots() * 2
        core = (lax.axis_index("tensor") % 2).astype(jnp.int32)
        mine, other = (chip + core) * tok, (chip + 1 - core) * tok
        place = lax.axis_index("pipe").astype(jnp.int32).reshape(1)
        return jnp.concatenate([mine[:1], other[:1], mine[1:], other[1:], place])

    def to_core(self, x):
        return lax.ppermute(x, "tensor", [(t, t ^ 1) for t in range(self.tensor)])

    def to_pipe(self, x, bit):
        return lax.ppermute(x, "pipe", [(i, i ^ bit) for i in range(self.pipe)])

    def to_next(self, x):
        pairs = [(self.ring[i], self.ring[(i + 1) % self.chips]) for i in range(self.chips)]
        return lax.ppermute(x, "tensor", [(2 * a + k, 2 * b + k) for a, b in pairs for k in range(2)])


def reduce_over_pipe(axes, partial):
    place = lax.axis_index("pipe")
    bits = axes.pipe.bit_length() - 1
    rows, cols = partial.shape
    left = partial.reshape((2,) * bits + (rows // axes.pipe, cols))
    for i in range(bits):
        axis = bits - 1 - i
        here = (place >> i) % 2
        send = lax.dynamic_slice_in_dim(left, 1 - here, 1, axis).astype(BF16)
        keep = lax.dynamic_slice_in_dim(left, here, 1, axis)
        left = keep + axes.to_pipe(send, 1 << i).astype(F32)
    held = {0: left.reshape(rows // axes.pipe, cols).astype(BF16)}
    for i in reversed(range(bits)):
        for r in list(held):
            held[r ^ (1 << i)] = axes.to_pipe(held[r], 1 << i)
    return [(held[r], r, 0) for r in range(axes.pipe)]


class Square:
    def __init__(self, axes, partial):
        self.axes, self.partial = axes, partial
        self.part = partial.shape[0] // 4
        self.half = self.part // 2

    def block(self, r, first, count):
        at = ((lax.axis_index("pipe") ^ r) * self.part + first, 0)
        return lax.dynamic_slice(self.partial, at, (count, self.partial.shape[1]))

    def send(self, for_1, for_2, others):
        for_1, for_2 = lax.optimization_barrier((for_1, for_2, *others))[:2] if others else (for_1, for_2)
        self.sent = (for_1, for_2)
        return self.axes.to_pipe(for_1, 1), self.axes.to_pipe(for_2, 2)

    def corner(self, others):
        half = self.half
        self.by = self.send(self.block(3, 0, half).astype(BF16), self.block(3, half, half).astype(BF16), others)

    def sides(self, others):
        half = self.half
        by_1, by_2 = [a.astype(F32) for a in self.by]
        for_1 = jnp.concatenate([self.block(1, 0, half), self.block(1, half, half) + by_2], axis=0).astype(BF16)
        for_2 = jnp.concatenate([self.block(2, 0, half) + by_1, self.block(2, half, half)], axis=0).astype(BF16)
        self.terms = self.send(for_1, for_2, others)

    def back(self, zero=0.0):
        mine = self.block(0, 0, self.part) + self.terms[0].astype(F32) + self.terms[1].astype(F32)
        self.mine = (mine + zero).astype(BF16)
        self.others = [(self.axes.to_pipe(self.mine, r), r, 0) for r in (1, 2, 3)]

    def result(self):
        return [(self.mine, 0, 0), *self.others]


def sigmoid(g):
    return 0.5 + 0.5 * jnp.tanh(0.5 * g)


def grads_kernel(cfg, at_rows, *refs):
    count = len(cfg["sources"])
    parts = refs[:count]
    gate_pre, up_pre, gate_w, up_w, gate_m, up_m = refs[count : count + 6]
    acc_in = refs[count + 6 : count + 10] if cfg["acc_in"] else None
    out, *acc, hidden, both = refs[-7:]
    step, tok, chunk = cfg["step"], cfg["tok"], cfg["chunk"]
    place = at_rows[cfg["groups"]]

    for (r, first), ref in zip(cfg["sources"], parts):
        to = (place ^ r) * cfg["part"] + first
        hidden[pl.ds(pl.multiple_of(to, 16), ref.shape[0]), :] = ref[...]
    for i in range(cfg["groups"]):
        at = pl.ds(pl.multiple_of(at_rows[i], 16), tok)
        rows = slice(i * tok, (i + 1) * tok)
        g = gate_pre[at, :].astype(F32)
        u = up_pre[at, :].astype(F32)
        h = hidden[rows, :].astype(F32)
        sig = sigmoid(g)
        h = h * sig
        gg = (h * u * (1.0 + g * (1.0 - sig))).astype(BF16)
        ug = (h * g).astype(BF16)
        out[at, :step] = gg
        out[at, step:] = ug
        both[rows, :step] = gg
        both[rows, step:] = ug

    @pl.when(pl.program_id(0) == 0)
    def _():
        for i, ref in enumerate(acc):
            ref[...] = jnp.zeros_like(ref) if acc_in is None else acc_in[i][...]

    def masked(w, m, at):
        rows = [
            w[at + i : at + i + BLOCK, :] * m[(at + i) // BLOCK : (at + i) // BLOCK + 1, :].astype(BF16)
            for i in range(0, chunk, BLOCK)
        ]
        return jnp.concatenate(rows, axis=0)

    for at in range(0, cfg["width"], chunk):
        w = jnp.concatenate([masked(gate_w, gate_m, at), masked(up_w, up_m, at)], axis=1)
        term = lax.dot_general(both[...], w, NT, preferred_element_type=F32)
        lo = 0
        for ref in acc:
            ref[:, at : at + chunk] += term[lo : lo + ref.shape[0], :]
            lo += ref.shape[0]


def local_grads(axes, at_rows, sources, gate_pre, up_pre, gate_w, up_w, gate_m, up_m, acc, tok, start, cols, ties):
    tokens, hid = gate_pre.shape
    width = gate_w.shape[0]
    step = step_of(hid)
    first = start // step
    col = lambda k, _: (0, first + k)
    one = lambda k, _: (0, 0)
    own = lambda k, _: (0, k)
    groups = [tok, tok, tokens // 2 - tok, tokens // 2 - tok]
    specs = [pl.BlockSpec((a.shape[0], step), own) for a, _, _ in sources]
    specs += [pl.BlockSpec((tokens, step), col)] * 2
    specs += [pl.BlockSpec((width, step), col)] * 2
    specs += [pl.BlockSpec((gate_m.shape[0], step), col)] * 2
    arrays = [a for a, _, _ in sources] + [gate_pre, up_pre, gate_w, up_w, gate_m, up_m]
    if acc is not None:
        specs += [pl.BlockSpec((n, width), one, pipeline_mode=pl.Buffered(1)) for n in groups]
        arrays += acc
    specs += [pl.BlockSpec(memory_space=pl.ANY)] * len(ties)
    arrays += ties
    cfg = dict(
        sources=[(r, lo) for _, r, lo in sources], part=tokens // axes.pipe, groups=tokens // tok, tok=tok, step=step,
        width=width, chunk=chunk_of(width, 1024), acc_in=acc is not None,
    )
    out = pl.pallas_call(
        functools.partial(grads_kernel, cfg),
        out_shape=[jax.ShapeDtypeStruct((tokens, 2 * cols), BF16)]
        + [jax.ShapeDtypeStruct((n, width), F32) for n in groups],
        grid_spec=pltpu.PrefetchScalarGridSpec(
            num_scalar_prefetch=1,
            grid=(cols // step,),
            in_specs=specs,
            out_specs=[pl.BlockSpec((tokens, 2 * step), own)] + [pl.BlockSpec((n, width), one) for n in groups],
            scratch_shapes=[pltpu.VMEM((tokens, step), BF16), pltpu.VMEM((tokens, 2 * step), BF16)],
        ),
        compiler_params=params(),
        cost_estimate=pl.CostEstimate(
            flops=4 * tokens * width * cols,
            bytes_accessed=4 * width * cols + 10 * tokens * cols + 8 * tokens * width,
            transcendentals=tokens * cols,
        ),
        name="local_grads",
    )(at_rows, *arrays)
    return out[0], list(out[1:])


def weights_kernel(cfg, x, grads, gate_m, up_m, *refs):
    gate_out, up_out, done = refs[-3:]
    done[...] = jnp.zeros_like(done)
    chunk, step = cfg["chunk"], cfg["step"]
    for at in range(0, cfg["width"], chunk):
        term = lax.dot_general(x[at : at + chunk, :], grads[...], NN, preferred_element_type=F32)
        for i in range(0, chunk, BLOCK):
            rows = slice(at + i, at + i + BLOCK)
            block = (at + i) // BLOCK
            gate_out[rows, :] = (term[i : i + BLOCK, :step] * gate_m[block : block + 1, :]).astype(BF16)
            up_out[rows, :] = (term[i : i + BLOCK, step:] * up_m[block : block + 1, :]).astype(BF16)


def weight_grads(x_t, grads, gate_m, up_m, before, shape, start, skip, steps, ties):
    width, tokens = x_t.shape
    step = step_of(shape[1])
    first = start // step + skip
    col = lambda k: (0, first + k)
    specs = [
        pl.BlockSpec((width, tokens), lambda k: (0, 0), pipeline_mode=pl.Buffered(1)),
        pl.BlockSpec((tokens, 2 * step), lambda k: (0, skip + k)),
        pl.BlockSpec((gate_m.shape[0], step), col),
        pl.BlockSpec((gate_m.shape[0], step), col),
    ]
    arrays = [x_t, grads, gate_m, up_m]
    alias = {}
    if before is not None:
        specs += [pl.BlockSpec(memory_space=pl.ANY)] * 2
        arrays += list(before)
        alias = {4: 0, 5: 1}
    specs += [pl.BlockSpec(memory_space=pl.ANY)] * len(ties)
    arrays += ties
    *out, done = pl.pallas_call(
        functools.partial(weights_kernel, dict(width=width, chunk=chunk_of(width, 512), step=step)),
        out_shape=[jax.ShapeDtypeStruct(shape, BF16)] * 2 + [jax.ShapeDtypeStruct((8, 128), F32)],
        grid=(steps,),
        in_specs=specs,
        out_specs=[pl.BlockSpec((width, step), col)] * 2 + [pl.BlockSpec((8, 128), lambda k: (0, 0))],
        input_output_aliases=alias,
        compiler_params=params(),
        cost_estimate=pl.CostEstimate(
            flops=4 * tokens * width * steps * step,
            bytes_accessed=4 * (width + tokens) * steps * step + 2 * tokens * width,
            transcendentals=0,
        ),
        name="weight_grads",
    )(*arrays)
    return out, done


def down_kernel(cfg, at_rows, *refs):
    rows, gate_pre, up_pre, mask = refs[:4]
    out, done, hidden = refs[-3:]
    tok = cfg["tok"]
    done[...] = jnp.zeros_like(done)
    for i in range(cfg["groups"]):
        at = pl.ds(pl.multiple_of(at_rows[i], 16), tok)
        g = gate_pre[at, :].astype(F32)
        u = up_pre[at, :].astype(F32)
        hidden[i * tok : (i + 1) * tok, :] = (g * sigmoid(g) * u).astype(BF16)
    across = hidden[...].T
    chunk = cfg["chunk"]

    for lo in range(0, cfg["width"], chunk):
        at = slice(lo, lo + chunk)
        term = lax.dot_general(across, rows[:, at], NN, preferred_element_type=F32)
        for i in range(cfg["step"] // BLOCK):
            part = slice(i * BLOCK, (i + 1) * BLOCK)
            out[part, at] = (term[part, :] * mask[i, :, at]).astype(BF16)


def down_grad(at_rows, rows, gate_pre, up_pre, mask, tok, before, first, last, ties):
    tokens, hid = gate_pre.shape
    width = rows.shape[1]
    step = step_of(hid)
    cfg = dict(groups=tokens // tok, tok=tok, width=width, step=step, chunk=chunk_of(width, 1024))
    specs = [pl.BlockSpec(rows.shape, lambda k, _: (0, 0), pipeline_mode=pl.Buffered(1))]
    specs += [pl.BlockSpec((tokens, step), lambda k, _: (0, first + k))] * 2
    specs += [pl.BlockSpec((step // BLOCK, 1, width), lambda k, _: (first + k, 0, 0))]
    arrays = [rows, gate_pre, up_pre, mask]
    alias = {}
    if before is not None:
        specs.append(pl.BlockSpec(memory_space=pl.ANY))
        arrays.append(before)
        alias = {len(arrays): 0}
    specs += [pl.BlockSpec(memory_space=pl.ANY)] * len(ties)
    arrays += ties
    cols = (last - first) * step
    return pl.pallas_call(
        functools.partial(down_kernel, cfg),
        out_shape=[jax.ShapeDtypeStruct((hid, width), BF16), jax.ShapeDtypeStruct((8, 128), F32)],
        grid_spec=pltpu.PrefetchScalarGridSpec(
            num_scalar_prefetch=1,
            grid=(last - first,),
            in_specs=specs,
            out_specs=[
                pl.BlockSpec((step, width), lambda k, _: (first + k, 0)),
                pl.BlockSpec((8, 128), lambda k, _: (0, 0)),
            ],
            scratch_shapes=[pltpu.VMEM((tokens, step), BF16)],
        ),
        input_output_aliases=alias,
        compiler_params=params(),
        cost_estimate=pl.CostEstimate(
            flops=2 * tokens * width * cols,
            bytes_accessed=2 * (tokens * width + 2 * tokens * cols + width * cols),
            transcendentals=tokens * cols,
        ),
        name="down_grad",
    )(at_rows, *arrays)


def masked(weight, mask):
    rows, cols = weight.shape
    return (weight.reshape(rows // BLOCK, BLOCK, cols) * mask.astype(BF16)[:, None, :]).reshape(rows, cols)


def dot_nt(a, b):
    return lax.dot_general(a, b, NT, preferred_element_type=F32)


def shards(axes, layer_input, out_grad, gate_pre, up_pre, gate_weight, up_weight, down_weight, gate_mask, up_mask, down_mask):
    tokens, hid = gate_pre.shape
    tok, width = out_grad.shape
    step = step_of(hid)
    steps = hid // step
    counts = [2, steps - 4, 2] if steps > 4 else [steps]
    pieces = [(sum(counts[:i]) * step, n * step) for i, n in enumerate(counts)]
    at_rows = axes.rows(tok)
    gate_m = jnp.repeat(gate_mask, BLOCK, axis=1).astype(F32)
    up_m = jnp.repeat(up_mask, BLOCK, axis=1).astype(F32)
    down_m = jnp.repeat(down_mask, BLOCK, axis=1).astype(F32)

    near = [out_grad, axes.to_core(out_grad)]
    down_part = lambda c, w, m: masked(down_weight[c : c + w], m[c // BLOCK : (c + w) // BLOCK])
    downs = [down_part(*pieces[0], down_m)]
    half = tok // 2
    now, got = [out_grad[:half], out_grad[half:]], []
    for s in range(axes.chips - 1):
        if s == 1:
            later = after(down_m, now[0])
            now[1] = after(now[1], *downs)
            downs += [down_part(c, w, later) for c, w in pieces[1:]]
        if s == 2:
            now[1] = after(now[1], *downs[1:])
        now = [axes.to_next(a) for a in now]
        got += now
    if len(downs) < len(pieces):
        downs += [down_part(c, w, down_m) for c, w in pieces[1:]]
    rows = jnp.concatenate(near + got + [axes.to_core(a) for a in got], axis=0)

    x = lax.all_gather(after(layer_input, rows), "tensor", axis=0, tiled=True)
    down = functools.partial(down_grad, rows=rows, gate_pre=gate_pre, up_pre=up_pre, mask=down_m[:, None, :], tok=tok)
    half_steps = (steps + 1) // 2
    if axes.pipe == 4:
        squares, waits = [], []
        for i, d in enumerate(downs):
            prev = squares[i - 1] if i else None
            sq = Square(axes, dot_nt(after(rows, *waits) if i else rows, d))
            squares.append(sq)
            sq.corner(prev.by if i else [])
            waits = sq.sent
            sq.sides(prev.terms if i else [])
            if i == 0 and len(downs) > 2:
                first_sides = sq.sent
            if i == 1:
                waits = first_sides if len(downs) > 2 else []
                grad_down, done = down(at_rows, before=None, first=0, last=half_steps, ties=[prev.mine, sq.sent[1]])
            sq.back(done[0, 0] if i == 1 else 0.0)
        sums = [sq.result() for sq in squares]
    else:
        sums = [reduce_over_pipe(axes, dot_nt(rows, d)) for d in downs]
        grad_down, done = down(at_rows, before=None, first=0, last=half_steps, ties=[])
    x_t = x.T

    acc, grads, weights, waits = None, [], None, []
    for i, ((c, w), sources) in enumerate(zip(pieces, sums)):
        if i + 1 < len(sums):
            waits = waits + [sums[i + 1][0][0]]
            if i + 2 < len(sums) and axes.pipe == 4:
                waits.append(squares[i + 2].sent[0])
        both, acc = local_grads(
            axes, at_rows, sources, gate_pre, up_pre, gate_weight, up_weight, gate_m, up_m, acc, tok, c, w, waits
        )
        grads.append(both)
        waits = []
        if not i:
            weights, ready = weight_grads(
                x_t, both, gate_m, up_m, None, gate_weight.shape, c, 0, w // step, [sums[-1][0][0]]
            )
            waits = [ready]

    todo = [(i, skip) for i in reversed(range(1, len(pieces))) for skip in range(0, pieces[i][1] // step, 2)]
    todo.insert(1, None)

    def next_part(ties):
        nonlocal weights, grad_down
        part = todo.pop(0)
        if part is None:
            grad_down, _ = down(at_rows, before=grad_down, first=half_steps, last=steps, ties=ties)
            return
        i, skip = part
        c, w = pieces[i]
        weights, _ = weight_grads(
            x_t, grads[i], gate_m, up_m, weights, gate_weight.shape, c, skip, min(2, w // step - skip), ties
        )

    near_own, near_other, far_own, far_other = acc
    far_there, near_there = axes.to_core(far_other), axes.to_core(near_other)
    next_part([])
    run = (far_own[:tok] + far_there[:tok]).astype(BF16)
    for s in range(1, axes.chips):
        if todo:
            next_part([run])
        at = slice(s * tok, (s + 1) * tok)
        term = far_own[at] + far_there[at] if s < axes.chips - 1 else near_own + near_there
        run = (axes.to_next(run).astype(F32) + term).astype(BF16)
    while todo:
        next_part([])
    return (run, weights[0], weights[1], grad_down)


def solution(mesh):
    in_specs = (
        P("tensor", "pipe"),
        P("tensor", "pipe"),
        P(None, "tensor"),
        P(None, "tensor"),
        P("pipe", "tensor"),
        P("pipe", "tensor"),
        P("tensor", "pipe"),
        P("pipe", "tensor"),
        P("pipe", "tensor"),
        P("tensor", "pipe"),
    )
    out_specs = (P("tensor", "pipe"), P("pipe", "tensor"), P("pipe", "tensor"), P("tensor", "pipe"))
    return jax.shard_map(
        functools.partial(shards, Axes(mesh)), mesh=mesh, in_specs=in_specs, out_specs=out_specs, check_vma=False
    )
```

```python
import functools

import jax
import jax.numpy as jnp
from jax import lax
from jax.experimental import pallas as pl
from jax.experimental.pallas import tpu as pltpu
from jax.sharding import PartitionSpec as P

BLOCK = 128
BF16 = jnp.bfloat16
F32 = jnp.float32
VMEM_BYTES = 60 * 1024 * 1024
NT = (((1,), (1,)), ((), ()))
NN = (((1,), (0,)), ((), ()))


def params():
    return pltpu.CompilerParams(vmem_limit_bytes=VMEM_BYTES)


def after(x, *others):
    return lax.optimization_barrier((x, *others))[0]


def nothing(x):
    return x[(0,) * x.ndim].astype(F32) * 0.0


def step_of(hid):
    return 512 if hid % 512 == 0 else 256


def chunk_of(size, most):
    return max(c for c in (128, 256, 512, 1024) if size % c == 0 and c <= most)


def ring_of(chips):
    return [0] + list(range(1, chips, 2)) + [c for c in range(chips - 1, 0, -1) if c % 2 == 0]


class Axes:
    def __init__(self, mesh):
        self.pipe = mesh.shape["pipe"]
        self.tensor = mesh.shape["tensor"]
        self.chips = self.tensor // 2
        self.ring = ring_of(self.chips)

    def slots(self):
        n = self.chips
        table = [[self.ring[(self.ring.index(c) - s) % n] for s in range(n)] for c in range(n)]
        return lax.dynamic_slice(jnp.array(table, jnp.int32), (lax.axis_index("tensor") // 2, 0), (1, n))[0]

    def rows(self, tok):
        chip = self.slots() * 2
        core = (lax.axis_index("tensor") % 2).astype(jnp.int32)
        mine, other = (chip + core) * tok, (chip + 1 - core) * tok
        place = lax.axis_index("pipe").astype(jnp.int32).reshape(1)
        return jnp.concatenate([mine[:1], other[:1], mine[1:], other[1:], place])

    def to_core(self, x):
        return lax.ppermute(x, "tensor", [(t, t ^ 1) for t in range(self.tensor)])

    def to_pipe(self, x, bit):
        return lax.ppermute(x, "pipe", [(i, i ^ bit) for i in range(self.pipe)])

    def to_next(self, x):
        pairs = [(self.ring[i], self.ring[(i + 1) % self.chips]) for i in range(self.chips)]
        return lax.ppermute(x, "tensor", [(2 * a + k, 2 * b + k) for a, b in pairs for k in range(2)])


def reduce_over_pipe(axes, partial):
    place = lax.axis_index("pipe")
    bits = axes.pipe.bit_length() - 1
    rows, cols = partial.shape
    left = partial.reshape((2,) * bits + (rows // axes.pipe, cols))
    for i in range(bits):
        axis = bits - 1 - i
        here = (place >> i) % 2
        send = lax.dynamic_slice_in_dim(left, 1 - here, 1, axis).astype(BF16)
        keep = lax.dynamic_slice_in_dim(left, here, 1, axis)
        left = keep + axes.to_pipe(send, 1 << i).astype(F32)
    held = {0: left.reshape(rows // axes.pipe, cols).astype(BF16)}
    for i in reversed(range(bits)):
        for r in list(held):
            held[r ^ (1 << i)] = axes.to_pipe(held[r], 1 << i)
    return [(held[r], r, 0) for r in range(axes.pipe)]


class Square:
    def __init__(self, axes, partial):
        self.axes, self.partial = axes, partial
        self.part = partial.shape[0] // 4
        self.half = self.part // 2

    def block(self, r, first, count):
        at = ((lax.axis_index("pipe") ^ r) * self.part + first, 0)
        return lax.dynamic_slice(self.partial, at, (count, self.partial.shape[1]))

    def send(self, for_1, for_2, others):
        for_1, for_2 = lax.optimization_barrier((for_1, for_2, *others))[:2] if others else (for_1, for_2)
        self.sent = (for_1, for_2)
        return self.axes.to_pipe(for_1, 1), self.axes.to_pipe(for_2, 2)

    def corner(self, others, zero=0.0):
        for_1, for_2 = self.block(3, 0, self.half) + zero, self.block(3, self.half, self.half) + zero
        self.by = self.send(for_1.astype(BF16), for_2.astype(BF16), others)

    def sides(self, others):
        half = self.half
        by_1, by_2 = [a.astype(F32) for a in self.by]
        for_1 = jnp.concatenate([self.block(1, 0, half), self.block(1, half, half) + by_2], axis=0).astype(BF16)
        for_2 = jnp.concatenate([self.block(2, 0, half) + by_1, self.block(2, half, half)], axis=0).astype(BF16)
        self.terms = self.send(for_1, for_2, others)

    def back(self, zero=0.0):
        mine = self.block(0, 0, self.part) + self.terms[0].astype(F32) + self.terms[1].astype(F32)
        self.mine = (mine + zero).astype(BF16)
        self.others = [(self.axes.to_pipe(self.mine, r), r, 0) for r in (1, 2, 3)]

    def result(self):
        return [(self.mine, 0, 0), *self.others]


def sigmoid(g):
    return 0.5 + 0.5 * jnp.tanh(0.5 * g)


def grads_kernel(cfg, at_rows, *refs):
    count = len(cfg["sources"])
    parts = refs[:count]
    gate_pre, up_pre, gate_w, up_w, gate_m, up_m = refs[count : count + 6]
    acc_in = refs[count + 6 : count + 10] if cfg["acc_in"] else None
    out, *acc, hidden, both = refs[-7:]
    step, tok, chunk = cfg["step"], cfg["tok"], cfg["chunk"]
    place = at_rows[cfg["groups"]]

    for (r, first), ref in zip(cfg["sources"], parts):
        to = (place ^ r) * cfg["part"] + first
        hidden[pl.ds(pl.multiple_of(to, 16), ref.shape[0]), :] = ref[...]
    for i in range(cfg["groups"]):
        at = pl.ds(pl.multiple_of(at_rows[i], 16), tok)
        rows = slice(i * tok, (i + 1) * tok)
        g = gate_pre[at, :].astype(F32)
        u = up_pre[at, :].astype(F32)
        h = hidden[rows, :].astype(F32)
        sig = sigmoid(g)
        h = h * sig
        gg = (h * u * (1.0 + g * (1.0 - sig))).astype(BF16)
        ug = (h * g).astype(BF16)
        out[at, :step] = gg
        out[at, step:] = ug
        both[rows, :step] = gg
        both[rows, step:] = ug

    @pl.when(pl.program_id(0) == 0)
    def _():
        for i, ref in enumerate(acc):
            ref[...] = jnp.zeros_like(ref) if acc_in is None else acc_in[i][...]

    def masked(w, m, at):
        rows = [
            w[at + i : at + i + BLOCK, :] * m[(at + i) // BLOCK : (at + i) // BLOCK + 1, :].astype(BF16)
            for i in range(0, chunk, BLOCK)
        ]
        return jnp.concatenate(rows, axis=0)

    for at in range(0, cfg["width"], chunk):
        w = jnp.concatenate([masked(gate_w, gate_m, at), masked(up_w, up_m, at)], axis=1)
        term = lax.dot_general(both[...], w, NT, preferred_element_type=F32)
        lo = 0
        for ref in acc:
            ref[:, at : at + chunk] += term[lo : lo + ref.shape[0], :]
            lo += ref.shape[0]


def local_grads(axes, at_rows, sources, gate_pre, up_pre, gate_w, up_w, gate_m, up_m, acc, tok, start, cols, ties):
    tokens, hid = gate_pre.shape
    width = gate_w.shape[0]
    step = step_of(hid)
    first = start // step
    col = lambda k, _: (0, first + k)
    one = lambda k, _: (0, 0)
    own = lambda k, _: (0, k)
    groups = [tok, tok, tokens // 2 - tok, tokens // 2 - tok]
    specs = [pl.BlockSpec((a.shape[0], step), own) for a, _, _ in sources]
    specs += [pl.BlockSpec((tokens, step), col)] * 2
    specs += [pl.BlockSpec((width, step), col)] * 2
    specs += [pl.BlockSpec((gate_m.shape[0], step), col)] * 2
    arrays = [a for a, _, _ in sources] + [gate_pre, up_pre, gate_w, up_w, gate_m, up_m]
    if acc is not None:
        specs += [pl.BlockSpec((n, width), one, pipeline_mode=pl.Buffered(1)) for n in groups]
        arrays += acc
    specs += [pl.BlockSpec(memory_space=pl.ANY)] * len(ties)
    arrays += ties
    cfg = dict(
        sources=[(r, lo) for _, r, lo in sources], part=tokens // axes.pipe, groups=tokens // tok, tok=tok, step=step,
        width=width, chunk=chunk_of(width, 1024), acc_in=acc is not None,
    )
    out = pl.pallas_call(
        functools.partial(grads_kernel, cfg),
        out_shape=[jax.ShapeDtypeStruct((tokens, 2 * cols), BF16)]
        + [jax.ShapeDtypeStruct((n, width), F32) for n in groups],
        grid_spec=pltpu.PrefetchScalarGridSpec(
            num_scalar_prefetch=1,
            grid=(cols // step,),
            in_specs=specs,
            out_specs=[pl.BlockSpec((tokens, 2 * step), own)] + [pl.BlockSpec((n, width), one) for n in groups],
            scratch_shapes=[pltpu.VMEM((tokens, step), BF16), pltpu.VMEM((tokens, 2 * step), BF16)],
        ),
        compiler_params=params(),
        cost_estimate=pl.CostEstimate(
            flops=4 * tokens * width * cols,
            bytes_accessed=4 * width * cols + 10 * tokens * cols + 8 * tokens * width,
            transcendentals=tokens * cols,
        ),
        name="local_grads",
    )(at_rows, *arrays)
    return out[0], list(out[1:])


def weights_kernel(cfg, x, grads, gate_m, up_m, *refs):
    gate_out, up_out, done = refs[-3:]
    done[...] = jnp.zeros_like(done)
    chunk, step = cfg["chunk"], cfg["step"]
    for at in range(0, cfg["width"], chunk):
        term = lax.dot_general(x[at : at + chunk, :], grads[...], NN, preferred_element_type=F32)
        for i in range(0, chunk, BLOCK):
            rows = slice(at + i, at + i + BLOCK)
            block = (at + i) // BLOCK
            gate_out[rows, :] = (term[i : i + BLOCK, :step] * gate_m[block : block + 1, :]).astype(BF16)
            up_out[rows, :] = (term[i : i + BLOCK, step:] * up_m[block : block + 1, :]).astype(BF16)


def weight_grads(x_t, grads, gate_m, up_m, before, shape, start, skip, steps, ties):
    width, tokens = x_t.shape
    step = step_of(shape[1])
    first = start // step + skip
    col = lambda k: (0, first + k)
    specs = [
        pl.BlockSpec((width, tokens), lambda k: (0, 0), pipeline_mode=pl.Buffered(1)),
        pl.BlockSpec((tokens, 2 * step), lambda k: (0, skip + k)),
        pl.BlockSpec((gate_m.shape[0], step), col),
        pl.BlockSpec((gate_m.shape[0], step), col),
    ]
    arrays = [x_t, grads, gate_m, up_m]
    alias = {}
    if before is not None:
        specs += [pl.BlockSpec(memory_space=pl.ANY)] * 2
        arrays += list(before)
        alias = {4: 0, 5: 1}
    specs += [pl.BlockSpec(memory_space=pl.ANY)] * len(ties)
    arrays += ties
    *out, done = pl.pallas_call(
        functools.partial(weights_kernel, dict(width=width, chunk=chunk_of(width, 512), step=step)),
        out_shape=[jax.ShapeDtypeStruct(shape, BF16)] * 2 + [jax.ShapeDtypeStruct((8, 128), F32)],
        grid=(steps,),
        in_specs=specs,
        out_specs=[pl.BlockSpec((width, step), col)] * 2 + [pl.BlockSpec((8, 128), lambda k: (0, 0))],
        input_output_aliases=alias,
        compiler_params=params(),
        cost_estimate=pl.CostEstimate(
            flops=4 * tokens * width * steps * step,
            bytes_accessed=4 * (width + tokens) * steps * step + 2 * tokens * width,
            transcendentals=0,
        ),
        name="weight_grads",
    )(*arrays)
    return out, done


def down_kernel(cfg, at_rows, *refs):
    rows, gate_pre, up_pre, mask = refs[:4]
    out, done, hidden = refs[-3:]
    tok = cfg["tok"]
    done[...] = jnp.zeros_like(done)
    for i in range(cfg["groups"]):
        at = pl.ds(pl.multiple_of(at_rows[i], 16), tok)
        g = gate_pre[at, :].astype(F32)
        u = up_pre[at, :].astype(F32)
        hidden[i * tok : (i + 1) * tok, :] = (g * sigmoid(g) * u).astype(BF16)
    across = hidden[...].T
    chunk = cfg["chunk"]

    for lo in range(0, cfg["width"], chunk):
        at = slice(lo, lo + chunk)
        term = lax.dot_general(across, rows[:, at], NN, preferred_element_type=F32)
        for i in range(cfg["step"] // BLOCK):
            part = slice(i * BLOCK, (i + 1) * BLOCK)
            out[part, at] = (term[part, :] * mask[i, :, at]).astype(BF16)


def down_grad(at_rows, rows, gate_pre, up_pre, mask, tok, before, first, last, ties):
    tokens, hid = gate_pre.shape
    width = rows.shape[1]
    step = step_of(hid)
    cfg = dict(groups=tokens // tok, tok=tok, width=width, step=step, chunk=chunk_of(width, 1024))
    specs = [pl.BlockSpec(rows.shape, lambda k, _: (0, 0), pipeline_mode=pl.Buffered(1))]
    specs += [pl.BlockSpec((tokens, step), lambda k, _: (0, first + k))] * 2
    specs += [pl.BlockSpec((step // BLOCK, 1, width), lambda k, _: (first + k, 0, 0))]
    arrays = [rows, gate_pre, up_pre, mask]
    alias = {}
    if before is not None:
        specs.append(pl.BlockSpec(memory_space=pl.ANY))
        arrays.append(before)
        alias = {len(arrays): 0}
    specs += [pl.BlockSpec(memory_space=pl.ANY)] * len(ties)
    arrays += ties
    cols = (last - first) * step
    return pl.pallas_call(
        functools.partial(down_kernel, cfg),
        out_shape=[jax.ShapeDtypeStruct((hid, width), BF16), jax.ShapeDtypeStruct((8, 128), F32)],
        grid_spec=pltpu.PrefetchScalarGridSpec(
            num_scalar_prefetch=1,
            grid=(last - first,),
            in_specs=specs,
            out_specs=[
                pl.BlockSpec((step, width), lambda k, _: (first + k, 0)),
                pl.BlockSpec((8, 128), lambda k, _: (0, 0)),
            ],
            scratch_shapes=[pltpu.VMEM((tokens, step), BF16)],
        ),
        input_output_aliases=alias,
        compiler_params=params(),
        cost_estimate=pl.CostEstimate(
            flops=2 * tokens * width * cols,
            bytes_accessed=2 * (tokens * width + 2 * tokens * cols + width * cols),
            transcendentals=tokens * cols,
        ),
        name="down_grad",
    )(at_rows, *arrays)


def masked(weight, mask):
    rows, cols = weight.shape
    return (weight.reshape(rows // BLOCK, BLOCK, cols) * mask.astype(BF16)[:, None, :]).reshape(rows, cols)


def dot_nt(a, b):
    return lax.dot_general(a, b, NT, preferred_element_type=F32)


def shards(axes, layer_input, out_grad, gate_pre, up_pre, gate_weight, up_weight, down_weight, gate_mask, up_mask, down_mask):
    tokens, hid = gate_pre.shape
    tok, width = out_grad.shape
    step = step_of(hid)
    steps = hid // step
    counts = [2, steps - 4, 2] if steps > 4 else [steps]
    pieces = [(sum(counts[:i]) * step, n * step) for i, n in enumerate(counts)]
    at_rows = axes.rows(tok)
    gate_m = jnp.repeat(gate_mask, BLOCK, axis=1).astype(F32)
    up_m = jnp.repeat(up_mask, BLOCK, axis=1).astype(F32)
    down_m = jnp.repeat(down_mask, BLOCK, axis=1).astype(F32)

    near = [out_grad, axes.to_core(out_grad)]
    down_part = lambda c, w, m: masked(down_weight[c : c + w], m[c // BLOCK : (c + w) // BLOCK])
    downs = [down_part(*pieces[0], down_m)]
    half = tok // 2
    now, got = [out_grad[:half], out_grad[half:]], []
    for s in range(axes.chips - 1):
        if s == 1:
            later = after(down_m, now[0])
            now[1] = after(now[1], *downs)
            downs += [down_part(c, w, later) for c, w in pieces[1:]]
        if s == 2:
            now[1] = after(now[1], *downs[1:])
        now = [axes.to_next(a) for a in now]
        got += now
    if len(downs) < len(pieces):
        downs += [down_part(c, w, down_m) for c, w in pieces[1:]]
    rows = jnp.concatenate(near + got + [axes.to_core(a) for a in got], axis=0)

    x = lax.all_gather(after(layer_input, rows), "tensor", axis=0, tiled=True)
    down = functools.partial(down_grad, rows=rows, gate_pre=gate_pre, up_pre=up_pre, mask=down_m[:, None, :], tok=tok)
    x_t = x.T

    def grads_of(i, sources, acc, ties):
        c, w = pieces[i]
        return local_grads(
            axes, at_rows, sources, gate_pre, up_pre, gate_weight, up_weight, gate_m, up_m, acc, tok, c, w, ties
        )

    def weights_of(i, both, before, skip, count, ties):
        return weight_grads(x_t, both, gate_m, up_m, before, gate_weight.shape, pieces[i][0], skip, count, ties)

    if axes.pipe == 4 and len(pieces) == 3:
        a = Square(axes, dot_nt(rows, downs[0]))
        a.corner([])
        b = Square(axes, dot_nt(after(rows, *a.sent), downs[1]))
        a.sides([])
        a_sides = a.sent
        b.corner(a.by)
        grad_down, done = down(at_rows, before=None, first=0, last=2, ties=[b.sent[0]])
        c = Square(axes, dot_nt(after(rows, *a_sides), downs[2]))
        c.corner(b.by, done[0, 0])
        a.back()
        b.sides(a.terms)
        b.back()
        c.sides(b.terms)
        grad_down, done = down(at_rows, before=grad_down, first=2, last=4, ties=[b.mine])
        both, acc = grads_of(0, a.result(), None, [b.mine, c.sent[0], done, x_t])
        grads = [both]
        weights, ready = weights_of(0, both, None, 0, 2, [])
        c.back(ready[0, 0])
        both, acc = grads_of(1, b.result(), acc, [c.mine])
        grads.append(both)
        both, acc = grads_of(2, c.result(), acc, [])
        grads.append(both)
    else:
        sums = [reduce_over_pipe(axes, dot_nt(rows, d)) for d in downs]
        grad_down, done = down(at_rows, before=None, first=0, last=min(4, steps), ties=[])
        acc, grads = None, []
        for i, sources in enumerate(sums):
            both, acc = grads_of(i, sources, acc, [])
            grads.append(both)
        weights, _ = weights_of(0, grads[0], None, 0, pieces[0][1] // step, [])

    todo = [(i, skip) for i in reversed(range(1, len(pieces))) for skip in range(0, pieces[i][1] // step, 2)]
    if steps > 4:
        todo.insert(1, None)

    def next_part(ties):
        nonlocal weights, grad_down
        part = todo.pop(0)
        if part is None:
            grad_down, _ = down(at_rows, before=grad_down, first=4, last=steps, ties=ties)
            return
        i, skip = part
        weights, _ = weights_of(i, grads[i], weights, skip, min(2, pieces[i][1] // step - skip), ties)

    near_own, near_other, far_own, far_other = acc
    far_there, near_there = axes.to_core(far_other), axes.to_core(near_other)
    next_part([])
    run = (far_own[:tok] + far_there[:tok]).astype(BF16)
    for s in range(1, axes.chips):
        if todo:
            next_part([run])
        at = slice(s * tok, (s + 1) * tok)
        term = far_own[at] + far_there[at] if s < axes.chips - 1 else near_own + near_there
        run = (axes.to_next(run).astype(F32) + term).astype(BF16)
    while todo:
        next_part([])
    return (run, weights[0], weights[1], grad_down)


def solution(mesh):
    in_specs = (
        P("tensor", "pipe"),
        P("tensor", "pipe"),
        P(None, "tensor"),
        P(None, "tensor"),
        P("pipe", "tensor"),
        P("pipe", "tensor"),
        P("tensor", "pipe"),
        P("pipe", "tensor"),
        P("pipe", "tensor"),
        P("tensor", "pipe"),
    )
    out_specs = (P("tensor", "pipe"), P("pipe", "tensor"), P("pipe", "tensor"), P("tensor", "pipe"))
    return jax.shard_map(
        functools.partial(shards, Axes(mesh)), mesh=mesh, in_specs=in_specs, out_specs=out_specs, check_vma=False
    )
```

```python
import functools

import jax
import jax.numpy as jnp
from jax import lax
from jax.experimental import pallas as pl
from jax.experimental.pallas import tpu as pltpu
from jax.sharding import PartitionSpec as P

BLOCK = 128
BF16 = jnp.bfloat16
F32 = jnp.float32
VMEM_BYTES = 60 * 1024 * 1024
NT = (((1,), (1,)), ((), ()))
NN = (((1,), (0,)), ((), ()))


def params():
    return pltpu.CompilerParams(vmem_limit_bytes=VMEM_BYTES)


def after(x, *others):
    return lax.optimization_barrier((x, *others))[0]


def nothing(x):
    return x[(0,) * x.ndim].astype(F32) * 0.0


def step_of(hid):
    return 512 if hid % 512 == 0 else 256


def chunk_of(size, most):
    return max(c for c in (128, 256, 512, 1024) if size % c == 0 and c <= most)


def ring_of(chips):
    return [0] + list(range(1, chips, 2)) + [c for c in range(chips - 1, 0, -1) if c % 2 == 0]


class Axes:
    def __init__(self, mesh):
        self.pipe = mesh.shape["pipe"]
        self.tensor = mesh.shape["tensor"]
        self.chips = self.tensor // 2
        self.ring = ring_of(self.chips)

    def slots(self):
        n = self.chips
        table = [[self.ring[(self.ring.index(c) - s) % n] for s in range(n)] for c in range(n)]
        return lax.dynamic_slice(jnp.array(table, jnp.int32), (lax.axis_index("tensor") // 2, 0), (1, n))[0]

    def rows(self, tok):
        chip = self.slots() * 2
        core = (lax.axis_index("tensor") % 2).astype(jnp.int32)
        mine, other = (chip + core) * tok, (chip + 1 - core) * tok
        place = lax.axis_index("pipe").astype(jnp.int32).reshape(1)
        return jnp.concatenate([mine[:1], other[:1], mine[1:], other[1:], place])

    def to_core(self, x):
        return lax.ppermute(x, "tensor", [(t, t ^ 1) for t in range(self.tensor)])

    def to_pipe(self, x, bit):
        return lax.ppermute(x, "pipe", [(i, i ^ bit) for i in range(self.pipe)])

    def to_next(self, x):
        pairs = [(self.ring[i], self.ring[(i + 1) % self.chips]) for i in range(self.chips)]
        return lax.ppermute(x, "tensor", [(2 * a + k, 2 * b + k) for a, b in pairs for k in range(2)])


def reduce_over_pipe(axes, partial):
    place = lax.axis_index("pipe")
    bits = axes.pipe.bit_length() - 1
    rows, cols = partial.shape
    left = partial.reshape((2,) * bits + (rows // axes.pipe, cols))
    for i in range(bits):
        axis = bits - 1 - i
        here = (place >> i) % 2
        send = lax.dynamic_slice_in_dim(left, 1 - here, 1, axis).astype(BF16)
        keep = lax.dynamic_slice_in_dim(left, here, 1, axis)
        left = keep + axes.to_pipe(send, 1 << i).astype(F32)
    held = {0: left.reshape(rows // axes.pipe, cols).astype(BF16)}
    for i in reversed(range(bits)):
        for r in list(held):
            held[r ^ (1 << i)] = axes.to_pipe(held[r], 1 << i)
    return [(held[r], r, 0) for r in range(axes.pipe)]


class Square:
    def __init__(self, axes, partial):
        self.axes, self.partial = axes, partial
        self.part = partial.shape[0] // 4
        self.half = self.part // 2

    def block(self, r, first, count):
        at = ((lax.axis_index("pipe") ^ r) * self.part + first, 0)
        return lax.dynamic_slice(self.partial, at, (count, self.partial.shape[1]))

    def send(self, for_1, for_2, others):
        for_1, for_2 = lax.optimization_barrier((for_1, for_2, *others))[:2] if others else (for_1, for_2)
        self.sent = (for_1, for_2)
        return self.axes.to_pipe(for_1, 1), self.axes.to_pipe(for_2, 2)

    def corner(self, others, zero=0.0):
        for_1, for_2 = self.block(3, 0, self.half) + zero, self.block(3, self.half, self.half) + zero
        self.by = self.send(for_1.astype(BF16), for_2.astype(BF16), others)

    def sides(self, others):
        half = self.half
        by_1, by_2 = [a.astype(F32) for a in self.by]
        for_1 = jnp.concatenate([self.block(1, 0, half), self.block(1, half, half) + by_2], axis=0).astype(BF16)
        for_2 = jnp.concatenate([self.block(2, 0, half) + by_1, self.block(2, half, half)], axis=0).astype(BF16)
        self.terms = self.send(for_1, for_2, others)

    def back(self, zero=0.0):
        mine = self.block(0, 0, self.part) + self.terms[0].astype(F32) + self.terms[1].astype(F32)
        self.mine = (mine + zero).astype(BF16)
        self.others = [(self.axes.to_pipe(self.mine, r), r, 0) for r in (1, 2, 3)]

    def result(self):
        return [(self.mine, 0, 0), *self.others]


def sigmoid(g):
    return 0.5 + 0.5 * jnp.tanh(0.5 * g)


def grads_kernel(cfg, at_rows, *refs):
    count = len(cfg["sources"])
    parts = refs[:count]
    gate_pre, up_pre, gate_w, up_w, gate_m, up_m = refs[count : count + 6]
    acc_in = refs[count + 6 : count + 10] if cfg["acc_in"] else None
    out, *acc, hidden, both = refs[-7:]
    step, tok, chunk = cfg["step"], cfg["tok"], cfg["chunk"]
    place = at_rows[cfg["groups"]]

    for (r, first), ref in zip(cfg["sources"], parts):
        to = (place ^ r) * cfg["part"] + first
        hidden[pl.ds(pl.multiple_of(to, 16), ref.shape[0]), :] = ref[...]
    for i in range(cfg["groups"]):
        at = pl.ds(pl.multiple_of(at_rows[i], 16), tok)
        rows = slice(i * tok, (i + 1) * tok)
        g = gate_pre[at, :].astype(F32)
        u = up_pre[at, :].astype(F32)
        h = hidden[rows, :].astype(F32)
        sig = sigmoid(g)
        h = h * sig
        gg = (h * u * (1.0 + g * (1.0 - sig))).astype(BF16)
        ug = (h * g).astype(BF16)
        out[at, :step] = gg
        out[at, step:] = ug
        both[rows, :step] = gg
        both[rows, step:] = ug

    @pl.when(pl.program_id(0) == 0)
    def _():
        for i, ref in enumerate(acc):
            ref[...] = jnp.zeros_like(ref) if acc_in is None else acc_in[i][...]

    def masked(w, m, at):
        rows = [
            w[at + i : at + i + BLOCK, :] * m[(at + i) // BLOCK : (at + i) // BLOCK + 1, :].astype(BF16)
            for i in range(0, chunk, BLOCK)
        ]
        return jnp.concatenate(rows, axis=0)

    for at in range(0, cfg["width"], chunk):
        w = jnp.concatenate([masked(gate_w, gate_m, at), masked(up_w, up_m, at)], axis=1)
        term = lax.dot_general(both[...], w, NT, preferred_element_type=F32)
        lo = 0
        for ref in acc:
            ref[:, at : at + chunk] += term[lo : lo + ref.shape[0], :]
            lo += ref.shape[0]


def local_grads(axes, at_rows, sources, gate_pre, up_pre, gate_w, up_w, gate_m, up_m, acc, tok, start, cols, ties):
    tokens, hid = gate_pre.shape
    width = gate_w.shape[0]
    step = step_of(hid)
    first = start // step
    col = lambda k, _: (0, first + k)
    one = lambda k, _: (0, 0)
    own = lambda k, _: (0, k)
    groups = [tok, tok, tokens // 2 - tok, tokens // 2 - tok]
    specs = [pl.BlockSpec((a.shape[0], step), own) for a, _, _ in sources]
    specs += [pl.BlockSpec((tokens, step), col)] * 2
    specs += [pl.BlockSpec((width, step), col)] * 2
    specs += [pl.BlockSpec((gate_m.shape[0], step), col)] * 2
    arrays = [a for a, _, _ in sources] + [gate_pre, up_pre, gate_w, up_w, gate_m, up_m]
    if acc is not None:
        specs += [pl.BlockSpec((n, width), one, pipeline_mode=pl.Buffered(1)) for n in groups]
        arrays += acc
    specs += [pl.BlockSpec(memory_space=pl.ANY)] * len(ties)
    arrays += ties
    cfg = dict(
        sources=[(r, lo) for _, r, lo in sources], part=tokens // axes.pipe, groups=tokens // tok, tok=tok, step=step,
        width=width, chunk=chunk_of(width, 1024), acc_in=acc is not None,
    )
    out = pl.pallas_call(
        functools.partial(grads_kernel, cfg),
        out_shape=[jax.ShapeDtypeStruct((tokens, 2 * cols), BF16)]
        + [jax.ShapeDtypeStruct((n, width), F32) for n in groups],
        grid_spec=pltpu.PrefetchScalarGridSpec(
            num_scalar_prefetch=1,
            grid=(cols // step,),
            in_specs=specs,
            out_specs=[pl.BlockSpec((tokens, 2 * step), own)] + [pl.BlockSpec((n, width), one) for n in groups],
            scratch_shapes=[pltpu.VMEM((tokens, step), BF16), pltpu.VMEM((tokens, 2 * step), BF16)],
        ),
        compiler_params=params(),
        cost_estimate=pl.CostEstimate(
            flops=4 * tokens * width * cols,
            bytes_accessed=4 * width * cols + 10 * tokens * cols + 8 * tokens * width,
            transcendentals=tokens * cols,
        ),
        name="local_grads",
    )(at_rows, *arrays)
    return out[0], list(out[1:])


def weights_kernel(cfg, x, grads, gate_m, up_m, *refs):
    gate_out, up_out, done = refs[-3:]
    done[...] = jnp.zeros_like(done)
    chunk, step = cfg["chunk"], cfg["step"]
    for at in range(0, cfg["width"], chunk):
        term = lax.dot_general(x[at : at + chunk, :], grads[...], NN, preferred_element_type=F32)
        for i in range(0, chunk, BLOCK):
            rows = slice(at + i, at + i + BLOCK)
            block = (at + i) // BLOCK
            gate_out[rows, :] = (term[i : i + BLOCK, :step] * gate_m[block : block + 1, :]).astype(BF16)
            up_out[rows, :] = (term[i : i + BLOCK, step:] * up_m[block : block + 1, :]).astype(BF16)


def weight_grads(x_t, grads, gate_m, up_m, before, shape, start, skip, steps, ties):
    width, tokens = x_t.shape
    step = step_of(shape[1])
    first = start // step + skip
    col = lambda k: (0, first + k)
    specs = [
        pl.BlockSpec((width, tokens), lambda k: (0, 0), pipeline_mode=pl.Buffered(1)),
        pl.BlockSpec((tokens, 2 * step), lambda k: (0, skip + k)),
        pl.BlockSpec((gate_m.shape[0], step), col),
        pl.BlockSpec((gate_m.shape[0], step), col),
    ]
    arrays = [x_t, grads, gate_m, up_m]
    alias = {}
    if before is not None:
        specs += [pl.BlockSpec(memory_space=pl.ANY)] * 2
        arrays += list(before)
        alias = {4: 0, 5: 1}
    specs += [pl.BlockSpec(memory_space=pl.ANY)] * len(ties)
    arrays += ties
    *out, done = pl.pallas_call(
        functools.partial(weights_kernel, dict(width=width, chunk=chunk_of(width, 512), step=step)),
        out_shape=[jax.ShapeDtypeStruct(shape, BF16)] * 2 + [jax.ShapeDtypeStruct((8, 128), F32)],
        grid=(steps,),
        in_specs=specs,
        out_specs=[pl.BlockSpec((width, step), col)] * 2 + [pl.BlockSpec((8, 128), lambda k: (0, 0))],
        input_output_aliases=alias,
        compiler_params=params(),
        cost_estimate=pl.CostEstimate(
            flops=4 * tokens * width * steps * step,
            bytes_accessed=4 * (width + tokens) * steps * step + 2 * tokens * width,
            transcendentals=0,
        ),
        name="weight_grads",
    )(*arrays)
    return out, done


def down_kernel(cfg, at_rows, *refs):
    rows, gate_pre, up_pre, mask = refs[:4]
    out, done, hidden = refs[-3:]
    tok = cfg["tok"]
    done[...] = jnp.zeros_like(done)
    for i in range(cfg["groups"]):
        at = pl.ds(pl.multiple_of(at_rows[i], 16), tok)
        g = gate_pre[at, :].astype(F32)
        u = up_pre[at, :].astype(F32)
        hidden[i * tok : (i + 1) * tok, :] = (g * sigmoid(g) * u).astype(BF16)
    across = hidden[...].T
    chunk = cfg["chunk"]

    for lo in range(0, cfg["width"], chunk):
        at = slice(lo, lo + chunk)
        term = lax.dot_general(across, rows[:, at], NN, preferred_element_type=F32)
        for i in range(cfg["step"] // BLOCK):
            part = slice(i * BLOCK, (i + 1) * BLOCK)
            out[part, at] = (term[part, :] * mask[i, :, at]).astype(BF16)


def down_grad(at_rows, rows, gate_pre, up_pre, mask, tok, before, first, last, ties):
    tokens, hid = gate_pre.shape
    width = rows.shape[1]
    step = step_of(hid)
    cfg = dict(groups=tokens // tok, tok=tok, width=width, step=step, chunk=chunk_of(width, 1024))
    specs = [pl.BlockSpec(rows.shape, lambda k, _: (0, 0), pipeline_mode=pl.Buffered(1))]
    specs += [pl.BlockSpec((tokens, step), lambda k, _: (0, first + k))] * 2
    specs += [pl.BlockSpec((step // BLOCK, 1, width), lambda k, _: (first + k, 0, 0))]
    arrays = [rows, gate_pre, up_pre, mask]
    alias = {}
    if before is not None:
        specs.append(pl.BlockSpec(memory_space=pl.ANY))
        arrays.append(before)
        alias = {len(arrays): 0}
    specs += [pl.BlockSpec(memory_space=pl.ANY)] * len(ties)
    arrays += ties
    cols = (last - first) * step
    return pl.pallas_call(
        functools.partial(down_kernel, cfg),
        out_shape=[jax.ShapeDtypeStruct((hid, width), BF16), jax.ShapeDtypeStruct((8, 128), F32)],
        grid_spec=pltpu.PrefetchScalarGridSpec(
            num_scalar_prefetch=1,
            grid=(last - first,),
            in_specs=specs,
            out_specs=[
                pl.BlockSpec((step, width), lambda k, _: (first + k, 0)),
                pl.BlockSpec((8, 128), lambda k, _: (0, 0)),
            ],
            scratch_shapes=[pltpu.VMEM((tokens, step), BF16)],
        ),
        input_output_aliases=alias,
        compiler_params=params(),
        cost_estimate=pl.CostEstimate(
            flops=2 * tokens * width * cols,
            bytes_accessed=2 * (tokens * width + 2 * tokens * cols + width * cols),
            transcendentals=tokens * cols,
        ),
        name="down_grad",
    )(at_rows, *arrays)


def masked(weight, mask):
    rows, cols = weight.shape
    return (weight.reshape(rows // BLOCK, BLOCK, cols) * mask.astype(BF16)[:, None, :]).reshape(rows, cols)


def dot_nt(a, b):
    return lax.dot_general(a, b, NT, preferred_element_type=F32)


def shards(axes, layer_input, out_grad, gate_pre, up_pre, gate_weight, up_weight, down_weight, gate_mask, up_mask, down_mask):
    tokens, hid = gate_pre.shape
    tok, width = out_grad.shape
    step = step_of(hid)
    steps = hid // step
    counts = [2, steps - 4, 2] if steps > 4 else [steps]
    pieces = [(sum(counts[:i]) * step, n * step) for i, n in enumerate(counts)]
    at_rows = axes.rows(tok)
    gate_m = jnp.repeat(gate_mask, BLOCK, axis=1).astype(F32)
    up_m = jnp.repeat(up_mask, BLOCK, axis=1).astype(F32)
    down_m = jnp.repeat(down_mask, BLOCK, axis=1).astype(F32)

    near = [out_grad, axes.to_core(out_grad)]
    down_part = lambda c, w, m: masked(down_weight[c : c + w], m[c // BLOCK : (c + w) // BLOCK])
    downs = [down_part(*pieces[0], down_m)]
    half = tok // 2
    now, got = [out_grad[:half], out_grad[half:]], []
    for s in range(axes.chips - 1):
        if s == 1:
            later = after(down_m, now[0])
            now[1] = after(now[1], *downs)
            downs += [down_part(c, w, later) for c, w in pieces[1:]]
        if s == 2:
            now[1] = after(now[1], *downs[1:])
        now = [axes.to_next(a) for a in now]
        got += now
    if len(downs) < len(pieces):
        downs += [down_part(c, w, down_m) for c, w in pieces[1:]]
    rows = jnp.concatenate(near + got + [axes.to_core(a) for a in got], axis=0)

    x = lax.all_gather(after(layer_input, rows), "tensor", axis=0, tiled=True)
    down = functools.partial(down_grad, rows=rows, gate_pre=gate_pre, up_pre=up_pre, mask=down_m[:, None, :], tok=tok)
    x_t = x.T

    def grads_of(i, sources, acc, ties):
        c, w = pieces[i]
        return local_grads(
            axes, at_rows, sources, gate_pre, up_pre, gate_weight, up_weight, gate_m, up_m, acc, tok, c, w, ties
        )

    def weights_of(i, both, before, skip, count, ties):
        return weight_grads(x_t, both, gate_m, up_m, before, gate_weight.shape, pieces[i][0], skip, count, ties)

    if axes.pipe == 4 and len(pieces) == 3:
        a = Square(axes, dot_nt(rows, downs[0]))
        a.corner([])
        b = Square(axes, dot_nt(after(rows, *a.sent), downs[1]))
        a.sides([])
        a_sides = a.sent
        b.corner(a.by)
        grad_down, done = down(at_rows, before=None, first=0, last=2, ties=[b.sent[0]])
        c = Square(axes, dot_nt(after(rows, *a_sides), downs[2]))
        c.corner(b.by, done[0, 0])
        a.back()
        b.sides(a.terms)
        grad_down, done = down(at_rows, before=grad_down, first=2, last=4, ties=[a.mine, *c.by])
        b.back()
        c.sides(b.terms)
        both, acc = grads_of(0, a.result(), None, [b.mine, c.sent[0], done, x_t])
        grads = [both]
        weights, ready = weights_of(0, both, None, 0, 2, [])
        c.back(ready[0, 0])
        both, acc = grads_of(1, b.result(), acc, [c.mine])
        grads.append(both)
        both, acc = grads_of(2, c.result(), acc, [])
        grads.append(both)
    else:
        sums = [reduce_over_pipe(axes, dot_nt(rows, d)) for d in downs]
        grad_down, done = down(at_rows, before=None, first=0, last=min(4, steps), ties=[])
        acc, grads = None, []
        for i, sources in enumerate(sums):
            both, acc = grads_of(i, sources, acc, [])
            grads.append(both)
        weights, _ = weights_of(0, grads[0], None, 0, pieces[0][1] // step, [])

    todo = list(reversed(range(1, len(pieces))))
    if steps > 4:
        todo.insert(1, None)

    def next_part(ties):
        nonlocal weights, grad_down
        part = todo.pop(0)
        if part is None:
            grad_down, _ = down(at_rows, before=grad_down, first=4, last=steps, ties=ties)
            return
        weights, _ = weights_of(part, grads[part], weights, 0, pieces[part][1] // step, ties)

    near_own, near_other, far_own, far_other = acc
    far_there, near_there = axes.to_core(far_other), axes.to_core(near_other)
    next_part([])
    run = (far_own[:tok] + far_there[:tok]).astype(BF16)
    for s in range(1, axes.chips):
        if todo:
            next_part([run])
        at = slice(s * tok, (s + 1) * tok)
        term = far_own[at] + far_there[at] if s < axes.chips - 1 else near_own + near_there
        run = (axes.to_next(run).astype(F32) + term).astype(BF16)
    while todo:
        next_part([])
    return (run, weights[0], weights[1], grad_down)


def solution(mesh):
    in_specs = (
        P("tensor", "pipe"),
        P("tensor", "pipe"),
        P(None, "tensor"),
        P(None, "tensor"),
        P("pipe", "tensor"),
        P("pipe", "tensor"),
        P("tensor", "pipe"),
        P("pipe", "tensor"),
        P("pipe", "tensor"),
        P("tensor", "pipe"),
    )
    out_specs = (P("tensor", "pipe"), P("pipe", "tensor"), P("pipe", "tensor"), P("tensor", "pipe"))
    return jax.shard_map(
        functools.partial(shards, Axes(mesh)), mesh=mesh, in_specs=in_specs, out_specs=out_specs, check_vma=False
    )
```
